128 devices in a mesh: frame: 32 (over x, y, core), row: 4 (over z).
Axes of the slice: x: 4, y: 4, z: 4, core: 2. Of those that a mesh axis runs over, the one named last changes fastest.
Arguments:
- hidden_in: bfloat16 [64, 1024, 1024], P('frame', 'row'), may hold values from -6 to 6
- query_weight: bfloat16 [1024, 1024], replicated, as said below
- kv_weight: bfloat16 [1024, 2048], replicated, may hold values from -0.1875 to 0.1875
- out_weight: bfloat16 [1024, 1024], replicated, may hold values from -0.1875 to 0.1875
- proj_in: bfloat16 [1024, 256], replicated, may hold values from -0.1875 to 0.1875
- proj_attn: bfloat16 [1024, 256], replicated, may hold values from -0.1875 to 0.1875
- camera_table: bfloat16 [6, 256], replicated, may hold values from -6 to 6
- camera_id: int32 [64], replicated, may hold values from 0 to 5
- t_query: bfloat16 [256, 256], replicated
- t_kv: bfloat16 [256, 512], replicated, may hold values from -0.375 to 0.375
- t_out: bfloat16 [256, 256], replicated, may hold values from -0.375 to 0.375
- depth_read: float32 [256], replicated, may hold values from -0.375 to 0.375
- lidar_pixel: int32 [64, 512], P('frame'), may hold values from 0 to 1023
- lidar_depth: float32 [64, 512], P('frame'), may hold values from 1 to 80
- lidar_valid: int32 [64, 512], P('frame'), may hold values from 0 to 1
Outputs:
- depth_map: float32 [64, 1024], P('frame', 'row')
- point_error: float32 [64, 512], P('frame')
- loss: float32 [], replicated
The draws below stay inside these ranges and needn't reach their ends.
Inputs may be any that keep to these rules, and one draw needn't show every extreme that they name: `query_weight`: query projection weights.
All inputs are finite; a program needn't handle non-finite values.
Results may differ from the reference program's by a relative error of at most 0.0085.
Values may be sent and summed in bfloat16 or wider, within the bound.
A program may use at most 128 MiB of HBM per device.

```python
import math
import jax
import jax.numpy as jnp
import numpy as np
from jax import lax

D = 1024
HEADS = 16
HW = 256
T_HEADS = 8
CAMERAS = 6
NPTS = 512
FRAMES = 64
PIXELS = 1024


def draw_query_weight(key, part):
    key = jax.random.fold_in(key, 11)
    values = jax.random.normal(key, (D, D), jnp.float32) * D ** (-0.5)
    return values.astype(jnp.bfloat16)


def draw_t_query(key, part):
    key = jax.random.fold_in(key, 12)
    values = jax.random.normal(key, (HW, HW), jnp.float32) * HW ** (-0.5)
    return values.astype(jnp.bfloat16)


def draw_lidar_valid(key, part):
    key = jax.random.fold_in(key, 13)
    span = FRAMES - 1
    ticket = jax.random.randint(key, (FRAMES, NPTS), 0, 4 * span)
    frame_pos = jnp.arange(FRAMES, dtype=jnp.int32)[:, None]
    return (ticket < span + 3 * frame_pos).astype(jnp.int32)


def set_ends(entries, rng, low, high):
    dims = entries.shape
    index_at = [jax.random.randint(jax.random.fold_in(rng, axis), (), 0, dims[axis]) for axis in range(len(dims))]
    entries = entries.at[tuple(index_at)].set(low)
    longest = dims.index(max(dims))
    index_at[longest] = (index_at[longest] + 1) % dims[longest]
    return entries.at[tuple(index_at)].set(high)


def level_of(stream_key, shape, pieces, smallest, top_value):
    level, own = 1.0, jax.random.fold_in(stream_key, 6)
    for axis_at, parts in pieces:
        steps = jnp.exp(jax.random.uniform(jax.random.fold_in(own, axis_at), (parts,), jnp.float32, smallest / len(pieces), top_value / len(pieces)))
        level = level * jnp.repeat(steps, shape[axis_at] // parts).reshape([-1 if axis == axis_at else 1 for axis in range(len(shape))])
    return level


def cumulative_ranks(number_of, slope):
    weights = [(1 << 20) // math.isqrt(rank ** slope) + 1 for rank in range(1, number_of + 1)]
    scale = 1 + sum(weights) // (1 << 30)
    return np.cumsum(np.array([max(1, weight // scale) for weight in weights]))


def ranked_ids(own_key, extent, amount, lean):
    table = cumulative_ranks(amount, lean)
    pick = jax.random.randint(jax.random.fold_in(own_key, 1), extent, 0, int(table[amount - 1]))
    rank = jnp.searchsorted(jnp.asarray(table, jnp.int32), pick, side="right")
    return jax.random.permutation(jax.random.fold_in(own_key, 2), amount)[rank].astype(jnp.int32)


def scatter_about(key, shape, spread, reach, cuts=(), kind=jnp.bfloat16):
    gain = level_of(key, shape, cuts, -0.22, 0.18) if cuts else 1.0
    values = jax.random.normal(key, shape, jnp.float32) * spread * gain
    return jnp.minimum(jnp.maximum(values, -reach), reach).astype(kind)


def setup_inputs(seed: int = 0) -> dict:
    seeds = jax.random.split(jax.random.key(seed), 16)
    return {
        "hidden_in": scatter_about(seeds[0], (FRAMES, PIXELS, D), 1.0, 6.0, ((0, 32), (1, 4))),
        "query_weight": draw_query_weight(jax.random.fold_in(seeds[15], 71), 0),
        "kv_weight": scatter_about(seeds[2], (D, 2 * D), D ** -0.5, 0.1875),
        "out_weight": scatter_about(seeds[3], (D, D), D ** -0.5, 0.1875),
        "proj_in": scatter_about(seeds[4], (D, HW), D ** -0.5, 0.1875),
        "proj_attn": scatter_about(seeds[5], (D, HW), D ** -0.5, 0.1875),
        "camera_table": scatter_about(seeds[6], (CAMERAS, HW), 1.0, 6.0),
        "camera_id": set_ends(jax.random.randint(seeds[7], (FRAMES,), 0, CAMERAS), jax.random.fold_in(seeds[7], 1), 0, CAMERAS - 1).astype(jnp.int32),
        "t_query": draw_t_query(jax.random.fold_in(seeds[15], 71), 0),
        "t_kv": scatter_about(seeds[9], (HW, 2 * HW), HW ** -0.5, 0.375),
        "t_out": scatter_about(seeds[10], (HW, HW), HW ** -0.5, 0.375),
        "depth_read": scatter_about(seeds[11], (HW,), HW ** -0.5, 0.375, (), jnp.float32),
        "lidar_pixel": set_ends(ranked_ids(seeds[12], (FRAMES, NPTS), PIXELS, 1), jax.random.fold_in(seeds[12], 3), 0, PIXELS - 1).astype(jnp.int32),
        "lidar_depth": jnp.clip(jnp.exp(math.log(80.0) - 4.3820266 * jax.random.uniform(seeds[13], (FRAMES, NPTS), jnp.float32) ** level_of(seeds[13], (FRAMES, NPTS), ((0, 32),), -0.2, 0.2)), 1.0, 80.0),
        "lidar_valid": draw_lidar_valid(jax.random.fold_in(seeds[15], 71), 0),
    }


def normalize(values):
    mean = lax.optimization_barrier(jnp.mean(values, axis=-1, keepdims=True))
    centred = values - mean
    var = lax.optimization_barrier(jnp.mean(centred * centred, axis=-1, keepdims=True))
    return centred * lax.rsqrt(var + 1e-06)

def reference(hidden_in, query_weight, kv_weight, out_weight, proj_in, proj_attn, camera_table, camera_id, t_query, t_kv, t_out, depth_read, lidar_pixel, lidar_depth, lidar_valid):
    head_dim = D // HEADS
    t_dim = HW // T_HEADS

    def encode(frame_rows):
        normed = normalize(frame_rows.astype(jnp.float32)).astype(jnp.bfloat16)
        query = jnp.dot(normed, query_weight, preferred_element_type=jnp.float32).astype(jnp.bfloat16)
        keyval = jnp.dot(normed, kv_weight, preferred_element_type=jnp.float32).astype(jnp.bfloat16)
        query = query.reshape(PIXELS, HEADS, head_dim).astype(jnp.float32)
        keys = keyval[:, :D].reshape(PIXELS, HEADS, head_dim).astype(jnp.float32)
        values = keyval[:, D:].reshape(PIXELS, HEADS, head_dim).astype(jnp.float32)
        scores = jnp.einsum('qhd,khd->hqk', query, keys) / math.sqrt(head_dim)
        probs = jnp.exp(scores - lax.optimization_barrier(jnp.max(scores, axis=-1, keepdims=True)))
        total = lax.optimization_barrier(jnp.sum(probs, axis=-1))
        numer = jnp.einsum('hqk,khd->hqd', probs.astype(jnp.bfloat16).astype(jnp.float32), values)
        attn = (numer / total[:, :, None]).astype(jnp.bfloat16)
        attn = jnp.transpose(attn, (1, 0, 2)).reshape(PIXELS, D)
        mixed = frame_rows.astype(jnp.float32) + jnp.dot(attn, out_weight, preferred_element_type=jnp.float32)
        after = normalize(mixed).astype(jnp.bfloat16)
        return (normed, after)
    hooks_a, hooks_b = lax.map(encode, hidden_in)
    onehot = (camera_id[:, None] == jnp.arange(CAMERAS, dtype=jnp.int32)[None, :]).astype(jnp.float32)
    cam_rows = jnp.dot(onehot, camera_table.astype(jnp.float32), precision=lax.Precision.HIGHEST)
    feat = jnp.dot(hooks_a.reshape(-1, D), proj_in, preferred_element_type=jnp.float32)
    feat = feat + jnp.dot(hooks_b.reshape(-1, D), proj_attn, preferred_element_type=jnp.float32)
    feat = (feat.reshape(FRAMES, PIXELS, HW) + cam_rows[:, None, :]).astype(jnp.bfloat16)
    normed_t = normalize(feat.astype(jnp.float32)).astype(jnp.bfloat16).reshape(-1, HW)
    tq = jnp.dot(normed_t, t_query, preferred_element_type=jnp.float32).astype(jnp.bfloat16)
    tkv = jnp.dot(normed_t, t_kv, preferred_element_type=jnp.float32).astype(jnp.bfloat16)
    tq = tq.reshape(FRAMES, PIXELS, T_HEADS, t_dim).astype(jnp.float32)
    tkv = tkv.reshape(FRAMES, PIXELS, 2 * HW)
    tk = tkv[:, :, :HW].reshape(FRAMES, PIXELS, T_HEADS, t_dim).astype(jnp.float32)
    tv = tkv[:, :, HW:].reshape(FRAMES, PIXELS, T_HEADS, t_dim).astype(jnp.float32)
    scores = jnp.einsum('tphd,sphd->phts', tq, tk) / math.sqrt(t_dim)
    probs = jnp.exp(scores - lax.optimization_barrier(jnp.max(scores, axis=-1, keepdims=True)))
    total = lax.optimization_barrier(jnp.sum(probs, axis=-1))
    numer = jnp.einsum('phts,sphd->tphd', probs.astype(jnp.bfloat16).astype(jnp.float32), tv)
    tattn = (numer / jnp.transpose(total, (2, 0, 1))[..., None]).astype(jnp.bfloat16).reshape(-1, HW)
    latent = feat.astype(jnp.float32).reshape(-1, HW) + jnp.dot(tattn, t_out, preferred_element_type=jnp.float32)
    depth_map = (0.1 + jax.nn.softplus(lax.optimization_barrier(jnp.sum(latent * depth_read, axis=-1)))).reshape(FRAMES, PIXELS)
    predicted = jnp.take_along_axis(depth_map, lidar_pixel, axis=1)
    valid = lidar_valid.astype(jnp.float32)
    point_error = valid * (jnp.log(predicted) - jnp.log(lidar_depth))
    loss = jnp.sum(jnp.abs(point_error)) / (FRAMES * NPTS)
    return (depth_map, point_error, loss)
```

```python
import functools
import math

import jax
import jax.numpy as jnp
from jax import lax
from jax.experimental import pallas as pl
from jax.experimental.pallas import tpu as pltpu
from jax.sharding import PartitionSpec as P

MESH = pl.DeviceIdType.MESH
BF = jnp.bfloat16
F32 = jnp.float32
LOG2E = 1.4426950408889634
T_HEADS = 8
CAMERAS = 6
NT = (((1,), (1,)), ((), ()))


def normalize(values):
    mean = jnp.mean(values, axis=-1, keepdims=True)
    centred = values - mean
    var = jnp.mean(centred * centred, axis=-1, keepdims=True)
    return centred * lax.rsqrt(var + 1e-06)


def dot(a, b):
    return jnp.dot(a, b, preferred_element_type=F32)


def lanes(shape):
    return lax.broadcasted_iota(jnp.int32, shape, len(shape) - 1)


def rows(shape):
    return lax.broadcasted_iota(jnp.int32, shape, len(shape) - 2)


def kernel(
    x_ref, wq_h, wkv_h, wo_h, pin_h, patt_h, cam_ref, cid_ref, tq_h, tkv_h, tout_h, dread_ref,
    lpix_ref, ldep_ref, lval_ref,
    depth_ref, perr_ref, loss_ref,
    hid, wq, wkv, wo, pin, patt, tqw, tkvw, toutw,
    normed, qm, kbuf, vbuf, sbuf0, sbuf1, attn, featin, fsend, frecv,
    perm, spread, tattn, lsend, lall, dsend, drecv, dfull,
    wsem, hid_s, hid_r, kv_s, kv_r, lid_s, lid_r, feat_s, feat_r, dep_s, dep_r,
):
    f = lax.axis_index("frame")
    z = lax.axis_index("row")
    j = f // 2
    c = f % 2
    t = 4 * j + z

    barrier = pltpu.get_barrier_semaphore()

    @pl.loop(0, 128)
    def _(i):
        @pl.when(i != 4 * f + z)
        def _():
            pl.semaphore_signal(
                barrier, inc=1, device_id=(i // 4, i % 4), device_id_type=MESH
            )

    weights = [
        pltpu.make_async_copy(src, dst, wsem.at[k])
        for k, (src, dst) in enumerate(
            [(wkv_h, wkv), (wq_h, wq), (pin_h, pin), (wo_h, wo), (patt_h, patt),
             (tq_h, tqw), (tkv_h, tkvw), (tout_h, toutw)]
        )
    ]
    for copy in weights:
        copy.start()

    for k in range(4):
        part = slice(128 * k, 128 * k + 128)
        pixel = jnp.where(lval_ref[:, part] != 0, lpix_ref[:, part], -1).astype(F32)
        lsend[2 * k : 2 * k + 2, :] = pixel
        lsend[8 + 2 * k : 10 + 2 * k, :] = jnp.log(ldep_ref[:, part])
    own_points = pltpu.make_async_copy(lsend, lall.at[f], lid_r)
    own_points.start()

    pl.semaphore_wait(barrier, 127)

    def piece_copy(i, h):
        return pltpu.make_async_remote_copy(
            src_ref=x_ref.at[i, pl.ds(128 * h, 128)],
            dst_ref=hid.at[z],
            send_sem=hid_s.at[2 * i + h],
            recv_sem=hid_r.at[z],
            device_id=(2 * j + h, 2 * c + i),
            device_id_type=MESH,
        )

    def piece_here(i, h):
        return (2 * c + i == z) & (h == c)

    pieces = [(i, h) for i in range(2) for h in range(2)]
    for i, h in pieces:

        @pl.when(jnp.logical_not(piece_here(i, h)))
        def _():
            piece_copy(i, h).start()

        @pl.when(piece_here(i, h))
        def _():
            pltpu.make_async_copy(
                x_ref.at[i, pl.ds(128 * h, 128)], hid.at[z], hid_r.at[z]
            ).start()

    def points_copy(ff):
        return pltpu.make_async_remote_copy(
            src_ref=lsend,
            dst_ref=lall.at[f],
            send_sem=lid_s,
            recv_sem=lid_r,
            device_id=(ff, z),
            device_id_type=MESH,
        )

    @pl.loop(0, 32)
    def _(ff):
        @pl.when(ff != f)
        def _():
            points_copy(ff).start()

    row = rows((512, 512))
    perm[...] = jnp.where(lanes((512, 512)) == (row % 64) * 8 + row // 64, 1.0, 0.0).astype(BF)
    row = rows((256, 64))
    spread[...] = jnp.where(lanes((256, 64)) == 2 * (row // 8) + row % 2, 1.0, 0.0)

    def swap(buf, piece, k):
        return pltpu.make_async_remote_copy(
            src_ref=buf.at[pl.ds(128 * piece, 128)],
            dst_ref=buf.at[pl.ds(512 + 128 * piece, 128)],
            send_sem=kv_s.at[k, piece],
            recv_sem=kv_r.at[k, piece],
            device_id=(2 * j + 1 - c, z),
            device_id_type=MESH,
        )

    low = lanes((128, 1024)) % 128 < 64
    for copy in weights[:3]:
        copy.wait()

    @pl.loop(0, 4)
    def _(step):
        far = jnp.where(step == 2, 3, jnp.where(step == 3, 2, step))
        piece = (z + far) % 4
        pltpu.make_async_copy(hid.at[piece], hid.at[piece], hid_r.at[piece]).wait()
        n = normalize(hid[piece].astype(F32)).astype(BF)
        at = pl.ds(pl.multiple_of(128 * piece, 128), 128)
        normed[at, :] = n
        kbuf[at, :] = dot(normed[at, :], wkv[:, :1024]).astype(BF)
        swap(kbuf, piece, 0).start()
        vbuf[at, :] = dot(normed[at, :], wkv[:, 1024:]).astype(BF)
        swap(vbuf, piece, 1).start()
        q = dot(normed[at, :], wq[...]) * (LOG2E / 8.0)
        qm[0, at, :] = jnp.where(low, q, 0.0).astype(BF)
        qm[1, at, :] = jnp.where(low, 0.0, q).astype(BF)
        featin[at, :] = dot(normed[at, :], pin[...])

    camera = cid_ref[t]
    cam_row = jnp.zeros((1, 256), F32)
    for k in range(CAMERAS):
        cam_row = cam_row + cam_ref[k : k + 1, :].astype(F32) * jnp.where(camera == k, 1.0, 0.0)

    for piece in range(4):
        for k, buf in ((0, kbuf), (1, vbuf)):
            swap(buf, piece, k).wait_recv()
    for copy in weights[3:]:
        copy.wait()

    def scores(index, out):
        qc, pair = index // 8, index % 8
        at = pl.ds(pl.multiple_of(256 * qc, 256), 256)
        col = pl.ds(pl.multiple_of(128 * pair, 128), 128)
        q2 = qm[:, at, col].reshape(512, 128)
        out[...] = lax.dot_general(q2, kbuf[:, col], NT, preferred_element_type=F32)

    left = lanes((256, 128)) < 64
    ones = jnp.ones((1024, 128), BF)

    def attend(index, s_ref):
        qc, pair = index // 8, index % 8
        at = pl.ds(pl.multiple_of(256 * qc, 256), 256)
        col = pl.ds(pl.multiple_of(128 * pair, 128), 128)
        s = s_ref[...]
        p = jnp.exp2((s - jnp.max(s, axis=-1, keepdims=True)).astype(BF))
        o = dot(p, jnp.concatenate([vbuf[:, col], ones], axis=1))
        num = jnp.where(left, o[:256, :128], o[256:, :128])
        den = jnp.where(left, o[:256, 128:], o[256:, 128:])
        attn[at, col] = (num / den).astype(BF)

    def feat_copy(m):
        return pltpu.make_async_remote_copy(
            src_ref=fsend.at[m],
            dst_ref=frecv.at[t],
            send_sem=feat_s,
            recv_sem=feat_r,
            device_id=(2 * (m % 16) + c, m // 16),
            device_id_type=MESH,
        )

    mine = 16 * z + j
    scores(0, sbuf0)
    for qc in range(2):

        @pl.loop(0, 4)
        def _(step):
            index = 8 * qc + 2 * step
            scores(index + 1, sbuf1)
            attend(index, sbuf0)
            scores((index + 2) % 16, sbuf0)
            attend(index + 1, sbuf1)

        at = slice(256 * qc, 256 * qc + 256)
        own = hid[2 * qc : 2 * qc + 2].reshape(256, 1024).astype(F32)
        mixed = own + dot(attn[at, :], wo[...])
        after = normalize(mixed).astype(BF)
        feat = featin[at, :] + dot(after, patt[...]) + cam_row
        both = jnp.concatenate(
            [feat[:, :128].reshape(32, 8, 128), feat[:, 128:].reshape(32, 8, 128)], axis=1
        )
        fsend[32 * qc : 32 * qc + 32] = both.astype(BF)

        @pl.loop(32 * qc, 32 * qc + 32)
        def _(m):
            @pl.when(m != mine)
            def _():
                feat_copy(m).start()

            @pl.when(m == mine)
            def _():
                pltpu.make_async_copy(fsend.at[m], frecv.at[t], feat_r).start()

    pltpu.make_async_copy(frecv, frecv, feat_r).wait()

    got = frecv[...].astype(F32)
    got = jnp.concatenate(
        [got[:, :8, :].reshape(512, 128), got[:, 8:, :].reshape(512, 128)], axis=1
    ).astype(BF)
    feat = dot(perm[...], got)
    y = normalize(feat).astype(BF)
    tq = dot(y, tqw[...]) * (LOG2E / math.sqrt(32.0))
    tkv = dot(y, tkvw[...]).astype(BF)
    same = rows((512, 128)) // 64 % 2 == lanes((512, 128)) // 64
    head = lanes((128, 128)) // 32
    ones_t = jnp.ones((128, 128), BF)
    for b in range(4):
        for g in range(2):
            at = slice(128 * b, 128 * b + 128)
            col = slice(128 * g, 128 * g + 128)
            qb = tq[at, col]
            q4 = jnp.concatenate(
                [jnp.where(head == h, qb, 0.0).astype(BF) for h in range(4)], axis=0
            )
            s = lax.dot_general(q4, tkv[at, col], NT, preferred_element_type=F32)
            s = jnp.where(same, s, -jnp.inf)
            p = jnp.exp2(s - jnp.max(s, axis=-1, keepdims=True)).astype(BF)
            v = tkv[at, 256 + 128 * g : 384 + 128 * g]
            o = dot(p, jnp.concatenate([v, ones_t], axis=1))
            num = o[:128, :128]
            den = o[:128, 128:]
            for h in range(1, 4):
                num = jnp.where(head == h, o[128 * h : 128 * h + 128, :128], num)
                den = jnp.where(head == h, o[128 * h : 128 * h + 128, 128:], den)
            tattn[at, col] = (num / den).astype(BF)
    latent = feat + dot(tattn[...], toutw[...])
    logit = jnp.sum(latent * dread_ref[...], axis=-1, keepdims=True)

    lane = lanes((64, 128))
    block = jnp.zeros((64, 128), F32)
    for p in range(8):
        block = jnp.where(lane == 8 * j + p, logit[64 * p : 64 * p + 64, :], block)
    depth = 0.1 + jnp.maximum(block, 0.0) + jnp.log(1.0 + jnp.exp(-jnp.abs(block)))
    log_depth = jnp.dot(
        spread[...], jnp.log(depth), precision=lax.Precision.HIGHEST, preferred_element_type=F32
    )

    pltpu.make_async_copy(lall, lall, lid_r).wait()
    pixel = lall[:, :8, :].reshape(256, 128).astype(jnp.int32) - (256 * z + 128 * c)
    hit = (pixel >= 8 * j) & (pixel < 8 * j + 8)
    predicted = jnp.take_along_axis(log_depth, jnp.clip(pixel, 0, 127), axis=1)
    error = jnp.abs(predicted - lall[:, 8:, :].reshape(256, 128))
    partial = jnp.sum(jnp.where(hit, error, 0.0))

    mixed_out = jnp.where(lane // 8 == j, depth, partial)
    for k in range(64):
        dsend[k] = mixed_out[k : k + 1, :]

    slot = 2 * (16 * (2 * z + c) + j)

    def depth_copy(ff, zz):
        return pltpu.make_async_remote_copy(
            src_ref=dsend.at[pl.ds(2 * ff, 2)],
            dst_ref=drecv.at[pl.ds(slot, 2)],
            send_sem=dep_s,
            recv_sem=dep_r,
            device_id=(ff, zz),
            device_id_type=MESH,
        )

    @pl.loop(0, 128)
    def _(d):
        @pl.when(d != 4 * f + z)
        def _():
            depth_copy(d // 4, d % 4).start()

        @pl.when(d == 4 * f + z)
        def _():
            pltpu.make_async_copy(
                dsend.at[pl.ds(2 * f, 2)], drecv.at[pl.ds(slot, 2)], dep_r
            ).start()

    pltpu.make_async_copy(drecv, drecv, dep_r).wait()

    group = lanes((1, 128)) // 8
    total = jnp.zeros((1, 128), F32)
    for b in range(8):
        acc = [jnp.zeros((1, 128), F32) for _ in range(2)]
        for jj in range(16):
            for i in range(2):
                part = drecv[2 * (16 * b + jj) + i]
                acc[i] = jnp.where(group == jj, part, acc[i])
                if i == 0:
                    total = total + jnp.where(group == (jj + 1) % 16, part, 0.0)
        for i in range(2):
            dfull[2 * b + i] = acc[i]
    for h in range(2):
        for i in range(2):
            depth_ref[i : i + 1, 128 * h : 128 * h + 128] = dfull[2 * (2 * z + h) + i]
    loss_ref[...] = jnp.sum(total, axis=-1, keepdims=True) * (1.0 / (8 * 64 * 512))

    pixel = lsend[:8, :].astype(jnp.int32)
    odd = rows((8, 128)) % 2 == 1
    found = jnp.ones((8, 128), F32)
    for b in range(8):
        table = jnp.where(
            odd,
            jnp.broadcast_to(dfull[2 * b + 1], (8, 128)),
            jnp.broadcast_to(dfull[2 * b], (8, 128)),
        )
        local = pixel - 128 * b
        value = jnp.take_along_axis(table, jnp.clip(local, 0, 127), axis=1)
        found = jnp.where((local >= 0) & (local < 128), value, found)
    error = jnp.where(pixel >= 0, jnp.log(found) - lsend[8:, :], 0.0)
    for k in range(4):
        perr_ref[:, 128 * k : 128 * k + 128] = error[2 * k : 2 * k + 2, :]

    for i, h in pieces:

        @pl.when(jnp.logical_not(piece_here(i, h)))
        def _():
            piece_copy(i, h).wait_send()

    for piece in range(4):
        for k, buf in ((0, kbuf), (1, vbuf)):
            swap(buf, piece, k).wait_send()
    pltpu.make_async_copy(lall.at[pl.ds(0, 31)], lall.at[pl.ds(0, 31)], lid_s).wait()
    pltpu.make_async_copy(frecv.at[pl.ds(0, 63)], frecv.at[pl.ds(0, 63)], feat_s).wait()
    pltpu.make_async_copy(drecv.at[pl.ds(0, 254)], drecv.at[pl.ds(0, 254)], dep_s).wait()


def body(
    hidden_in, query_weight, kv_weight, out_weight, proj_in, proj_attn, camera_table, camera_id,
    t_query, t_kv, t_out, depth_read, lidar_pixel, lidar_depth, lidar_valid,
):
    hbm = pl.BlockSpec(memory_space=pl.ANY)
    vmem = pl.BlockSpec(memory_space=pltpu.VMEM)
    smem = pl.BlockSpec(memory_space=pltpu.SMEM)
    dma = pltpu.SemaphoreType.DMA
    depth_map, point_error, loss = pl.pallas_call(
        kernel,
        out_shape=(
            jax.ShapeDtypeStruct((2, 256), F32),
            jax.ShapeDtypeStruct((2, 512), F32),
            jax.ShapeDtypeStruct((1, 1), F32),
        ),
        in_specs=[
            hbm, hbm, hbm, hbm, hbm, hbm, vmem, smem, hbm, hbm, hbm, vmem, vmem, vmem, vmem,
        ],
        out_specs=(vmem, vmem, vmem),
        scratch_shapes=[
            pltpu.VMEM((4, 128, 1024), BF),
            pltpu.VMEM((1024, 1024), BF),
            pltpu.VMEM((1024, 2048), BF),
            pltpu.VMEM((1024, 1024), BF),
            pltpu.VMEM((1024, 256), BF),
            pltpu.VMEM((1024, 256), BF),
            pltpu.VMEM((256, 256), BF),
            pltpu.VMEM((256, 512), BF),
            pltpu.VMEM((256, 256), BF),
            pltpu.VMEM((512, 1024), BF),
            pltpu.VMEM((2, 512, 1024), BF),
            pltpu.VMEM((1024, 1024), BF),
            pltpu.VMEM((1024, 1024), BF),
            pltpu.VMEM((512, 1024), F32),
            pltpu.VMEM((512, 1024), F32),
            pltpu.VMEM((512, 1024), BF),
            pltpu.VMEM((512, 256), F32),
            pltpu.VMEM((64, 16, 128), BF),
            pltpu.VMEM((64, 16, 128), BF),
            pltpu.VMEM((512, 512), BF),
            pltpu.VMEM((256, 64), F32),
            pltpu.VMEM((512, 256), BF),
            pltpu.VMEM((16, 128), F32),
            pltpu.VMEM((32, 16, 128), F32),
            pltpu.VMEM((64, 1, 128), F32),
            pltpu.VMEM((256, 1, 128), F32),
            pltpu.VMEM((16, 1, 128), F32),
            dma((8,)), dma((4,)), dma((4,)), dma((2, 4)), dma((2, 4)),
            dma, dma, dma, dma, dma, dma,
        ],
        compiler_params=pltpu.CompilerParams(
            collective_id=0, has_side_effects=True, vmem_limit_bytes=56 * 2**20
        ),
        cost_estimate=pl.CostEstimate(
            flops=8_000_000_000, bytes_accessed=12_000_000, transcendentals=9_000_000
        ),
    )(
        hidden_in, query_weight, kv_weight, out_weight, proj_in, proj_attn, camera_table,
        camera_id, t_query, t_kv, t_out, depth_read.reshape(1, -1), lidar_pixel, lidar_depth,
        lidar_valid,
    )
    return depth_map, point_error, loss.reshape(())


def solution(mesh):
    return jax.shard_map(
        body,
        mesh=mesh,
        in_specs=(
            P("frame", "row", None),
            P(),
            P(),
            P(),
            P(),
            P(),
            P(),
            P(),
            P(),
            P(),
            P(),
            P(),
            P("frame", None),
            P("frame", None),
            P("frame", None),
        ),
        out_specs=(P("frame", "row"), P("frame", None), P()),
        check_vma=False,
    )
```

```python
import functools
import math

import jax
import jax.numpy as jnp
from jax import lax
from jax.experimental import pallas as pl
from jax.experimental.pallas import tpu as pltpu
from jax.sharding import PartitionSpec as P

MESH = pl.DeviceIdType.MESH
BF = jnp.bfloat16
F32 = jnp.float32
LOG2E = 1.4426950408889634
T_HEADS = 8
CAMERAS = 6
NT = (((1,), (1,)), ((), ()))


def normalize(values):
    mean = jnp.mean(values, axis=-1, keepdims=True)
    centred = values - mean
    var = jnp.mean(centred * centred, axis=-1, keepdims=True)
    return centred * lax.rsqrt(var + 1e-06)


def dot(a, b):
    return jnp.dot(a, b, preferred_element_type=F32)


def lanes(shape):
    return lax.broadcasted_iota(jnp.int32, shape, len(shape) - 1)


def rows(shape):
    return lax.broadcasted_iota(jnp.int32, shape, len(shape) - 2)


def kernel(
    x_ref, wq_h, wkv_h, wo_h, pin_h, patt_h, cam_ref, cid_ref, tq_h, tkv_h, tout_h, dread_ref,
    lpix_ref, ldep_ref, lval_ref,
    depth_ref, perr_ref, loss_ref,
    hid, wq, wkv, wo, pin, patt, tqw, tkvw, toutw,
    normed, qm, kbuf, vbuf, sbuf0, sbuf1, attn, featin, fsend, frecv,
    perm, spread, tattn, lsend, lall, dsend, drecv, dfull,
    here_x, here_y, wsem, hid_s, hid_r, kv_s, kv_r, lid_s, lid_r, feat_s, feat_r, dep_s, dep_r,
):
    f = lax.axis_index("frame")
    z = lax.axis_index("row")
    j = f // 2
    c = f % 2
    t = 4 * j + z

    barrier = pltpu.get_barrier_semaphore()

    gx, gy = f // 8, j % 4
    column = [(2 * j + (c + dc) % 2, (z + dz) % 4) for dz in range(4) for dc in range(2)][1:]
    along_x = [(8 * ((gx + d) % 4) + 2 * gy + c, z) for d in range(1, 4)]
    along_y = [(8 * gx + 2 * ((gy + d) % 4) + c, z) for d in range(1, 4)]
    for device in column + along_x + along_y:
        pl.semaphore_signal(barrier, inc=1, device_id=device, device_id_type=MESH)

    weights = [
        pltpu.make_async_copy(src, dst, wsem.at[k])
        for k, (src, dst) in enumerate(
            [(wkv_h, wkv), (wq_h, wq), (pin_h, pin), (wo_h, wo), (patt_h, patt),
             (tq_h, tqw), (tkv_h, tkvw), (tout_h, toutw)]
        )
    ]
    for copy in weights:
        copy.start()

    for k in range(4):
        part = slice(128 * k, 128 * k + 128)
        pixel = jnp.where(lval_ref[:, part] != 0, lpix_ref[:, part], -1).astype(F32)
        lsend[2 * k : 2 * k + 2, :] = pixel
        lsend[8 + 2 * k : 10 + 2 * k, :] = jnp.log(ldep_ref[:, part])
    own_points = pltpu.make_async_copy(lsend, lall.at[f], lid_r)
    own_points.start()

    pl.semaphore_wait(barrier, 13)

    def piece_copy(i, h):
        return pltpu.make_async_remote_copy(
            src_ref=x_ref.at[i, pl.ds(128 * h, 128)],
            dst_ref=hid.at[z],
            send_sem=hid_s.at[2 * i + h],
            recv_sem=hid_r.at[z],
            device_id=(2 * j + h, 2 * c + i),
            device_id_type=MESH,
        )

    def piece_here(i, h):
        return (2 * c + i == z) & (h == c)

    pieces = [(i, h) for i in range(2) for h in range(2)]
    for far in (False, True):
        for i, h in pieces:

            @pl.when(jnp.logical_not(piece_here(i, h)) & (((2 * c + i - z + 4) % 4 == 2) == far))
            def _():
                piece_copy(i, h).start()

    for i, h in pieces:

        @pl.when(piece_here(i, h))
        def _():
            pltpu.make_async_copy(
                x_ref.at[i, pl.ds(128 * h, 128)], hid.at[z], hid_r.at[z]
            ).start()

    for device in along_x:
        pl.semaphore_signal(here_x, inc=1, device_id=device, device_id_type=MESH)

    row = rows((512, 512))
    perm[...] = jnp.where(lanes((512, 512)) == (row % 64) * 8 + row // 64, 1.0, 0.0).astype(BF)
    row = rows((256, 64))
    spread[...] = jnp.where(lanes((256, 64)) == 2 * (row // 8) + row % 2, 1.0, 0.0)

    pl.semaphore_wait(here_x, 3)
    for device in along_y:
        pl.semaphore_signal(here_y, inc=1, device_id=device, device_id_type=MESH)

    def swap(buf, piece, k):
        return pltpu.make_async_remote_copy(
            src_ref=buf.at[pl.ds(128 * piece, 128)],
            dst_ref=buf.at[pl.ds(512 + 128 * piece, 128)],
            send_sem=kv_s.at[k, piece],
            recv_sem=kv_r.at[k, piece],
            device_id=(2 * j + 1 - c, z),
            device_id_type=MESH,
        )

    low = lanes((128, 1024)) % 128 < 64
    for copy in weights[:3]:
        copy.wait()

    def points_copy(ff):
        return pltpu.make_async_remote_copy(
            src_ref=lsend,
            dst_ref=lall.at[f],
            send_sem=lid_s,
            recv_sem=lid_r,
            device_id=(ff, z),
            device_id_type=MESH,
        )

    def project(piece):
        pltpu.make_async_copy(hid.at[piece], hid.at[piece], hid_r.at[piece]).wait()
        n = normalize(hid[piece].astype(F32)).astype(BF)
        at = pl.ds(pl.multiple_of(128 * piece, 128), 128)
        normed[at, :] = n
        kbuf[at, :] = dot(normed[at, :], wkv[:, :1024]).astype(BF)
        swap(kbuf, piece, 0).start()
        vbuf[at, :] = dot(normed[at, :], wkv[:, 1024:]).astype(BF)
        swap(vbuf, piece, 1).start()
        q = dot(normed[at, :], wq[...]) * (LOG2E / 8.0)
        qm[0, at, :] = jnp.where(low, q, 0.0).astype(BF)
        qm[1, at, :] = jnp.where(low, 0.0, q).astype(BF)
        featin[at, :] = dot(normed[at, :], pin[...])

    @pl.loop(0, 4)
    def _(step):
        far = jnp.where(step == 2, 3, jnp.where(step == 3, 2, step))
        project((z + far) % 4)

        @pl.when(step == 0)
        def _():
            pl.semaphore_wait(here_y, 3)

            @pl.loop(0, 32)
            def _(ff):
                @pl.when(ff != f)
                def _():
                    points_copy(ff).start()

    camera = cid_ref[t]
    cam_row = jnp.zeros((1, 256), F32)
    for k in range(CAMERAS):
        cam_row = cam_row + cam_ref[k : k + 1, :].astype(F32) * jnp.where(camera == k, 1.0, 0.0)

    for piece in range(4):
        for k, buf in ((0, kbuf), (1, vbuf)):
            swap(buf, piece, k).wait_recv()
    for copy in weights[3:]:
        copy.wait()

    def scores(index, out):
        qc, pair = index // 8, index % 8
        at = pl.ds(pl.multiple_of(256 * qc, 256), 256)
        col = pl.ds(pl.multiple_of(128 * pair, 128), 128)
        q2 = qm[:, at, col].reshape(512, 128)
        out[...] = lax.dot_general(q2, kbuf[:, col], NT, preferred_element_type=F32)

    left = lanes((256, 128)) < 64
    ones = jnp.ones((1024, 128), BF)

    def attend(index, s_ref):
        qc, pair = index // 8, index % 8
        at = pl.ds(pl.multiple_of(256 * qc, 256), 256)
        col = pl.ds(pl.multiple_of(128 * pair, 128), 128)
        s = s_ref[...]
        p = jnp.exp2((s - jnp.max(s, axis=-1, keepdims=True)).astype(BF))
        o = dot(p, jnp.concatenate([vbuf[:, col], ones], axis=1))
        num = jnp.where(left, o[:256, :128], o[256:, :128])
        den = jnp.where(left, o[:256, 128:], o[256:, 128:])
        attn[at, col] = (num / den).astype(BF)

    def feat_copy(m):
        return pltpu.make_async_remote_copy(
            src_ref=fsend.at[m],
            dst_ref=frecv.at[t],
            send_sem=feat_s,
            recv_sem=feat_r,
            device_id=(2 * (m % 16) + c, (m // 16 + 2) % 4),
            device_id_type=MESH,
        )

    block_row = (z + 2) % 4
    mine = 16 * block_row + j
    scores(0, sbuf0)
    for qc in range(2):

        @pl.loop(0, 4)
        def _(step):
            index = 8 * qc + 2 * step
            scores(index + 1, sbuf1)
            attend(index, sbuf0)
            scores((index + 2) % 16, sbuf0)
            attend(index + 1, sbuf1)

        at = slice(256 * qc, 256 * qc + 256)
        own = hid[2 * qc : 2 * qc + 2].reshape(256, 1024).astype(F32)
        mixed = own + dot(attn[at, :], wo[...])
        after = normalize(mixed).astype(BF)
        feat = featin[at, :] + dot(after, patt[...]) + cam_row
        both = jnp.concatenate(
            [feat[:, :128].reshape(32, 8, 128), feat[:, 128:].reshape(32, 8, 128)], axis=1
        )
        fsend[32 * qc : 32 * qc + 32] = both.astype(BF)

        @pl.loop(32 * qc, 32 * qc + 32)
        def _(m):
            @pl.when(m != mine)
            def _():
                feat_copy(m).start()

            @pl.when(m == mine)
            def _():
                pltpu.make_async_copy(fsend.at[m], frecv.at[t], feat_r).start()

    pltpu.make_async_copy(frecv, frecv, feat_r).wait()

    got = frecv[...].astype(F32)
    got = jnp.concatenate(
        [got[:, :8, :].reshape(512, 128), got[:, 8:, :].reshape(512, 128)], axis=1
    ).astype(BF)
    feat = dot(perm[...], got)
    y = normalize(feat).astype(BF)
    tq = dot(y, tqw[...]) * (LOG2E / math.sqrt(32.0))
    tkv = dot(y, tkvw[...]).astype(BF)
    same = rows((512, 128)) // 64 % 2 == lanes((512, 128)) // 64
    head = lanes((128, 128)) // 32
    ones_t = jnp.ones((128, 128), BF)
    for b in range(4):
        for g in range(2):
            at = slice(128 * b, 128 * b + 128)
            col = slice(128 * g, 128 * g + 128)
            qb = tq[at, col]
            q4 = jnp.concatenate(
                [jnp.where(head == h, qb, 0.0).astype(BF) for h in range(4)], axis=0
            )
            s = lax.dot_general(q4, tkv[at, col], NT, preferred_element_type=F32)
            s = jnp.where(same, s, -jnp.inf)
            p = jnp.exp2(s - jnp.max(s, axis=-1, keepdims=True)).astype(BF)
            v = tkv[at, 256 + 128 * g : 384 + 128 * g]
            o = dot(p, jnp.concatenate([v, ones_t], axis=1))
            num = o[:128, :128]
            den = o[:128, 128:]
            for h in range(1, 4):
                num = jnp.where(head == h, o[128 * h : 128 * h + 128, :128], num)
                den = jnp.where(head == h, o[128 * h : 128 * h + 128, 128:], den)
            tattn[at, col] = (num / den).astype(BF)
    latent = feat + dot(tattn[...], toutw[...])
    logit = jnp.sum(latent * dread_ref[...], axis=-1, keepdims=True)

    lane = lanes((64, 128))
    block = jnp.zeros((64, 128), F32)
    for p in range(8):
        block = jnp.where(lane == 8 * j + p, logit[64 * p : 64 * p + 64, :], block)
    depth = 0.1 + jnp.maximum(block, 0.0) + jnp.log(1.0 + jnp.exp(-jnp.abs(block)))
    log_depth = jnp.dot(
        spread[...], jnp.log(depth), precision=lax.Precision.HIGHEST, preferred_element_type=F32
    )

    pltpu.make_async_copy(lall, lall, lid_r).wait()
    pixel = lall[:, :8, :].reshape(256, 128).astype(jnp.int32) - (256 * block_row + 128 * c)
    hit = (pixel >= 8 * j) & (pixel < 8 * j + 8)
    predicted = jnp.take_along_axis(log_depth, jnp.clip(pixel, 0, 127), axis=1)
    error = jnp.abs(predicted - lall[:, 8:, :].reshape(256, 128))
    partial = jnp.sum(jnp.where(hit, error, 0.0))

    mixed_out = jnp.where(lane // 8 == j, depth, partial)
    for k in range(64):
        dsend[k] = mixed_out[k : k + 1, :]

    slot = 2 * (16 * (2 * block_row + c) + j)

    def depth_copy(ff, zz):
        return pltpu.make_async_remote_copy(
            src_ref=dsend.at[pl.ds(2 * ff, 2)],
            dst_ref=drecv.at[pl.ds(slot, 2)],
            send_sem=dep_s,
            recv_sem=dep_r,
            device_id=(ff, zz),
            device_id_type=MESH,
        )

    @pl.loop(0, 128)
    def _(d):
        @pl.when(d != 4 * f + z)
        def _():
            depth_copy(d // 4, d % 4).start()

        @pl.when(d == 4 * f + z)
        def _():
            pltpu.make_async_copy(
                dsend.at[pl.ds(2 * f, 2)], drecv.at[pl.ds(slot, 2)], dep_r
            ).start()

    pltpu.make_async_copy(drecv, drecv, dep_r).wait()

    group = lanes((1, 128)) // 8
    total = jnp.zeros((1, 128), F32)
    for b in range(8):
        acc = [jnp.zeros((1, 128), F32) for _ in range(2)]
        for jj in range(16):
            for i in range(2):
                part = drecv[2 * (16 * b + jj) + i]
                acc[i] = jnp.where(group == jj, part, acc[i])
                if i == 0:
                    total = total + jnp.where(group == (jj + 1) % 16, part, 0.0)
        for i in range(2):
            dfull[2 * b + i] = acc[i]
    for h in range(2):
        for i in range(2):
            depth_ref[i : i + 1, 128 * h : 128 * h + 128] = dfull[2 * (2 * z + h) + i]
    loss_ref[...] = jnp.sum(total, axis=-1, keepdims=True) * (1.0 / (8 * 64 * 512))

    pixel = lsend[:8, :].astype(jnp.int32)
    odd = rows((8, 128)) % 2 == 1
    found = jnp.ones((8, 128), F32)
    for b in range(8):
        table = jnp.where(
            odd,
            jnp.broadcast_to(dfull[2 * b + 1], (8, 128)),
            jnp.broadcast_to(dfull[2 * b], (8, 128)),
        )
        local = pixel - 128 * b
        value = jnp.take_along_axis(table, jnp.clip(local, 0, 127), axis=1)
        found = jnp.where((local >= 0) & (local < 128), value, found)
    error = jnp.where(pixel >= 0, jnp.log(found) - lsend[8:, :], 0.0)
    for k in range(4):
        perr_ref[:, 128 * k : 128 * k + 128] = error[2 * k : 2 * k + 2, :]

    for i, h in pieces:

        @pl.when(jnp.logical_not(piece_here(i, h)))
        def _():
            piece_copy(i, h).wait_send()

    for piece in range(4):
        for k, buf in ((0, kbuf), (1, vbuf)):
            swap(buf, piece, k).wait_send()
    pltpu.make_async_copy(lall.at[pl.ds(0, 31)], lall.at[pl.ds(0, 31)], lid_s).wait()
    pltpu.make_async_copy(frecv.at[pl.ds(0, 63)], frecv.at[pl.ds(0, 63)], feat_s).wait()
    pltpu.make_async_copy(drecv.at[pl.ds(0, 254)], drecv.at[pl.ds(0, 254)], dep_s).wait()


def pass_on(depth_in, perr_in, loss_in, depth_out, perr_out, loss_out):
    depth_out[...] = depth_in[...]
    perr_out[...] = perr_in[...]
    loss_out[...] = loss_in[...]


def body(
    hidden_in, query_weight, kv_weight, out_weight, proj_in, proj_attn, camera_table, camera_id,
    t_query, t_kv, t_out, depth_read, lidar_pixel, lidar_depth, lidar_valid,
):
    hbm = pl.BlockSpec(memory_space=pl.ANY)
    vmem = pl.BlockSpec(memory_space=pltpu.VMEM)
    smem = pl.BlockSpec(memory_space=pltpu.SMEM)
    dma = pltpu.SemaphoreType.DMA
    depth_map, point_error, loss = pl.pallas_call(
        kernel,
        out_shape=(
            jax.ShapeDtypeStruct((2, 256), F32),
            jax.ShapeDtypeStruct((2, 512), F32),
            jax.ShapeDtypeStruct((1, 1), F32),
        ),
        in_specs=[
            hbm, hbm, hbm, hbm, hbm, hbm, vmem, smem, hbm, hbm, hbm, vmem, vmem, vmem, vmem,
        ],
        out_specs=(vmem, vmem, vmem),
        scratch_shapes=[
            pltpu.VMEM((4, 128, 1024), BF),
            pltpu.VMEM((1024, 1024), BF),
            pltpu.VMEM((1024, 2048), BF),
            pltpu.VMEM((1024, 1024), BF),
            pltpu.VMEM((1024, 256), BF),
            pltpu.VMEM((1024, 256), BF),
            pltpu.VMEM((256, 256), BF),
            pltpu.VMEM((256, 512), BF),
            pltpu.VMEM((256, 256), BF),
            pltpu.VMEM((512, 1024), BF),
            pltpu.VMEM((2, 512, 1024), BF),
            pltpu.VMEM((1024, 1024), BF),
            pltpu.VMEM((1024, 1024), BF),
            pltpu.VMEM((512, 1024), F32),
            pltpu.VMEM((512, 1024), F32),
            pltpu.VMEM((512, 1024), BF),
            pltpu.VMEM((512, 256), F32),
            pltpu.VMEM((64, 16, 128), BF),
            pltpu.VMEM((64, 16, 128), BF),
            pltpu.VMEM((512, 512), BF),
            pltpu.VMEM((256, 64), F32),
            pltpu.VMEM((512, 256), BF),
            pltpu.VMEM((16, 128), F32),
            pltpu.VMEM((32, 16, 128), F32),
            pltpu.VMEM((64, 1, 128), F32),
            pltpu.VMEM((256, 1, 128), F32),
            pltpu.VMEM((16, 1, 128), F32),
            pltpu.SemaphoreType.REGULAR, pltpu.SemaphoreType.REGULAR,
            dma((8,)), dma((4,)), dma((4,)), dma((2, 4)), dma((2, 4)),
            dma, dma, dma, dma, dma, dma,
        ],
        compiler_params=pltpu.CompilerParams(
            collective_id=0, has_side_effects=True, vmem_limit_bytes=56 * 2**20
        ),
        cost_estimate=pl.CostEstimate(
            flops=8_000_000_000, bytes_accessed=12_000_000, transcendentals=9_000_000
        ),
    )(
        hidden_in, query_weight, kv_weight, out_weight, proj_in, proj_attn, camera_table,
        camera_id, t_query, t_kv, t_out, depth_read.reshape(1, -1), lidar_pixel, lidar_depth,
        lidar_valid,
    )
    depth_map, point_error, loss = pl.pallas_call(
        pass_on,
        out_shape=(
            jax.ShapeDtypeStruct((2, 256), F32),
            jax.ShapeDtypeStruct((2, 512), F32),
            jax.ShapeDtypeStruct((1, 1), F32),
        ),
        in_specs=[vmem, vmem, vmem],
        out_specs=(vmem, vmem, vmem),
    )(depth_map, point_error, loss)
    return depth_map, point_error, loss.reshape(())


def solution(mesh):
    return jax.shard_map(
        body,
        mesh=mesh,
        in_specs=(
            P("frame", "row", None),
            P(),
            P(),
            P(),
            P(),
            P(),
            P(),
            P(),
            P(),
            P(),
            P(),
            P(),
            P("frame", None),
            P("frame", None),
            P("frame", None),
        ),
        out_specs=(P("frame", "row"), P("frame", None), P()),
        check_vma=False,
    )
```

```python
import functools
import math

import jax
import jax.numpy as jnp
from jax import lax
from jax.experimental import pallas as pl
from jax.experimental.pallas import tpu as pltpu
from jax.sharding import PartitionSpec as P

MESH = pl.DeviceIdType.MESH
BF = jnp.bfloat16
F32 = jnp.float32
LOG2E = 1.4426950408889634
T_HEADS = 8
CAMERAS = 6
NT = (((1,), (1,)), ((), ()))


def normalize(values):
    mean = jnp.mean(values, axis=-1, keepdims=True)
    centred = values - mean
    var = jnp.mean(centred * centred, axis=-1, keepdims=True)
    return centred * lax.rsqrt(var + 1e-06)


def dot(a, b):
    return jnp.dot(a, b, preferred_element_type=F32)


def lanes(shape):
    return lax.broadcasted_iota(jnp.int32, shape, len(shape) - 1)


def rows(shape):
    return lax.broadcasted_iota(jnp.int32, shape, len(shape) - 2)


def kernel(
    x_ref, wq_h, wkv_h, wo_h, pin_h, patt_h, cam_ref, cid_ref, tq_h, tkv_h, tout_h, dread_ref,
    lpix_ref, ldep_ref, lval_ref,
    depth_ref, perr_ref, loss_ref,
    hid, wq, wkv, wo, pin, patt, tqw, tkvw, toutw,
    normed, qm, kbuf, vbuf, sbuf0, sbuf1, abuf0, abuf1, bbuf0, bbuf1, obuf, mbuf, attn, featin, fsend, frecv,
    perm, spread, tattn, lsend, lall, dsend, drecv, dfull,
    here_x, here_y, wsem, hid_s, hid_r, kv_s, kv_r, lid_s, lid_r, feat_s, feat_r, dep_s, dep_r,
):
    f = lax.axis_index("frame")
    z = lax.axis_index("row")
    j = f // 2
    c = f % 2
    t = 4 * j + z

    barrier = pltpu.get_barrier_semaphore()

    gx, gy = f // 8, j % 4
    column = [(2 * j + (c + dc) % 2, (z + dz) % 4) for dz in range(4) for dc in range(2)][1:]
    along_x = [(8 * ((gx + d) % 4) + 2 * gy + c, z) for d in range(1, 4)]
    along_y = [(8 * gx + 2 * ((gy + d) % 4) + c, z) for d in range(1, 4)]
    for device in column + along_x + along_y:
        pl.semaphore_signal(barrier, inc=1, device_id=device, device_id_type=MESH)

    weights = [
        pltpu.make_async_copy(src, dst, wsem.at[k])
        for k, (src, dst) in enumerate(
            [(wkv_h, wkv), (wq_h, wq), (pin_h, pin), (wo_h, wo), (patt_h, patt),
             (tq_h, tqw), (tkv_h, tkvw), (tout_h, toutw)]
        )
    ]
    for copy in weights:
        copy.start()

    for k in range(4):
        part = slice(128 * k, 128 * k + 128)
        pixel = jnp.where(lval_ref[:, part] != 0, lpix_ref[:, part], -1).astype(F32)
        lsend[2 * k : 2 * k + 2, :] = pixel
        lsend[8 + 2 * k : 10 + 2 * k, :] = jnp.log(ldep_ref[:, part])
    own_points = pltpu.make_async_copy(lsend, lall.at[f], lid_r)
    own_points.start()

    pl.semaphore_wait(barrier, 13)

    def slot_of(i):
        far = (z - 2 * c - i + 4) % 4
        return jnp.where(far == 2, 3, jnp.where(far == 3, 2, far))

    def piece_copy(i, h):
        return pltpu.make_async_remote_copy(
            src_ref=x_ref.at[i, pl.ds(128 * h, 128)],
            dst_ref=hid.at[slot_of(i)],
            send_sem=hid_s.at[2 * i + h],
            recv_sem=hid_r.at[slot_of(i)],
            device_id=(2 * j + h, 2 * c + i),
            device_id_type=MESH,
        )

    def piece_here(i, h):
        return (2 * c + i == z) & (h == c)

    pieces = [(i, h) for i in range(2) for h in range(2)]

    def is_far(i):
        return (2 * c + i - z + 4) % 4 == 2

    for i, h in pieces:

        @pl.when(jnp.logical_not(piece_here(i, h) | is_far(i)))
        def _():
            piece_copy(i, h).start()

    for i, h in pieces:

        @pl.when(piece_here(i, h))
        def _():
            pltpu.make_async_copy(
                x_ref.at[i, pl.ds(128 * h, 128)], hid.at[0], hid_r.at[0]
            ).start()

    for device in along_x:
        pl.semaphore_signal(here_x, inc=1, device_id=device, device_id_type=MESH)

    row = rows((512, 512))
    perm[...] = jnp.where(lanes((512, 512)) == (row % 64) * 8 + row // 64, 1.0, 0.0).astype(BF)
    row = rows((256, 64))
    spread[...] = jnp.where(lanes((256, 64)) == 2 * (row // 8) + row % 2, 1.0, 0.0)

    pl.semaphore_wait(here_x, 3)
    for device in along_y:
        pl.semaphore_signal(here_y, inc=1, device_id=device, device_id_type=MESH)

    def swap(buf, piece, k):
        return pltpu.make_async_remote_copy(
            src_ref=buf.at[pl.ds(256 * piece, 128)],
            dst_ref=buf.at[pl.ds(256 * piece + 128, 128)],
            send_sem=kv_s.at[k, piece],
            recv_sem=kv_r.at[k, piece],
            device_id=(2 * j + 1 - c, z),
            device_id_type=MESH,
        )

    low = lanes((128, 1024)) % 128 < 64
    for copy in weights[:3]:
        copy.wait()

    def points_copy(ff):
        return pltpu.make_async_remote_copy(
            src_ref=lsend,
            dst_ref=lall.at[f],
            send_sem=lid_s,
            recv_sem=lid_r,
            device_id=(ff, z),
            device_id_type=MESH,
        )

    def project(piece):
        pltpu.make_async_copy(hid.at[piece], hid.at[piece], hid_r.at[piece]).wait()
        n = normalize(hid[piece].astype(F32)).astype(BF)
        at = pl.ds(pl.multiple_of(128 * piece, 128), 128)
        keys = pl.ds(pl.multiple_of(256 * piece, 256), 128)
        normed[at, :] = n
        kbuf[keys, :] = dot(normed[at, :], wkv[:, :1024]).astype(BF)
        swap(kbuf, piece, 0).start()
        vbuf[keys, :] = dot(normed[at, :], wkv[:, 1024:]).astype(BF)
        swap(vbuf, piece, 1).start()
        q = dot(normed[at, :], wq[...]) * (LOG2E / 8.0)
        qm[0, at, :] = jnp.where(low, q, 0.0).astype(BF)
        qm[1, at, :] = jnp.where(low, 0.0, q).astype(BF)
        featin[at, :] = dot(normed[at, :], pin[...])

    @pl.loop(0, 3)
    def _(step):
        project(step)

        @pl.when(step == 0)
        def _():
            pl.semaphore_wait(here_y, 3)
            for i, h in pieces:

                @pl.when(jnp.logical_not(piece_here(i, h) | is_far(i)))
                def _():
                    piece_copy(i, h).wait_send()

            for i, h in pieces:

                @pl.when(is_far(i))
                def _():
                    piece_copy(i, h).start()

            @pl.loop(0, 32)
            def _(ff):
                @pl.when(ff != f)
                def _():
                    points_copy(ff).start()

    camera = cid_ref[t]
    cam_row = jnp.zeros((1, 256), F32)
    for k in range(CAMERAS):
        cam_row = cam_row + cam_ref[k : k + 1, :].astype(F32) * jnp.where(camera == k, 1.0, 0.0)

    for piece in range(3):
        for k, buf in ((0, kbuf), (1, vbuf)):
            swap(buf, piece, k).wait_recv()
    for copy in weights[3:]:
        copy.wait()

    def scores_first(pair, out):
        col = pl.ds(pl.multiple_of(128 * pair, 128), 128)
        q2 = qm[:, :384, col].reshape(768, 128)
        out[...] = lax.dot_general(q2, kbuf[:768, col], NT, preferred_element_type=F32)

    def values(at, col, count):
        return jnp.concatenate([vbuf[at, col], jnp.ones((count, 128), BF)], axis=1)

    def attend_first(pair, s_ref):
        col = pl.ds(pl.multiple_of(128 * pair, 128), 128)
        s = s_ref[...]
        top = jnp.max(s, axis=-1, keepdims=True)
        p = jnp.exp2((s - top).astype(BF))
        obuf[pair] = dot(p, values(slice(0, 768), col, 768))
        mbuf[pair] = jnp.broadcast_to(top, (768, 128))

    def scores_last(pair, out_a, out_b):
        col = pl.ds(pl.multiple_of(128 * pair, 128), 128)
        q2 = qm[:, :384, col].reshape(768, 128)
        out_a[...] = lax.dot_general(q2, kbuf[768:, col], NT, preferred_element_type=F32)
        q2 = qm[:, 384:, col].reshape(256, 128)
        out_b[...] = lax.dot_general(q2, kbuf[:, col], NT, preferred_element_type=F32)

    def heads_of(o, count):
        left = lanes((count, 128)) < 64
        num = jnp.where(left, o[:count, :128], o[count:, :128])
        den = jnp.where(left, o[:count, 128:], o[count:, 128:])
        return (num / den).astype(BF)

    def attend_last(pair, a_ref, b_ref):
        col = pl.ds(pl.multiple_of(128 * pair, 128), 128)
        s = a_ref[...]
        before = mbuf[pair]
        top = jnp.maximum(before, jnp.max(s, axis=-1, keepdims=True))
        p = jnp.exp2((s - jnp.concatenate([top, top], axis=1)).astype(BF))
        keep = jnp.exp2(before - top)
        o = obuf[pair] * jnp.concatenate([keep, keep], axis=1)
        o = o + dot(p, values(slice(768, 1024), col, 256))
        attn[:384, col] = heads_of(o, 384)
        s = b_ref[...]
        p = jnp.exp2((s - jnp.max(s, axis=-1, keepdims=True)).astype(BF))
        attn[384:, col] = heads_of(dot(p, values(slice(0, 1024), col, 1024)), 128)

    def row_of(piece):
        return (z + 2 + jnp.where(piece == 2, 3, jnp.where(piece == 3, 2, piece))) % 4

    def feat_copy(m):
        return pltpu.make_async_remote_copy(
            src_ref=fsend.at[m],
            dst_ref=frecv.at[t],
            send_sem=feat_s,
            recv_sem=feat_r,
            device_id=(2 * (m % 16) + c, row_of(m // 16)),
            device_id_type=MESH,
        )

    block_row = (z + 2) % 4
    mine = 48 + j
    scores_first(0, sbuf0)

    @pl.loop(0, 4)
    def _(step):
        @pl.when(step == 3)
        def _():
            project(3)

        pair = 2 * step
        scores_first(pair + 1, sbuf1)
        attend_first(pair, sbuf0)
        scores_first((pair + 2) % 8, sbuf0)
        attend_first(pair + 1, sbuf1)

    for k, buf in ((0, kbuf), (1, vbuf)):
        swap(buf, 3, k).wait_recv()
    scores_last(0, abuf0, bbuf0)

    @pl.loop(0, 4)
    def _(step):
        pair = 2 * step
        scores_last(pair + 1, abuf1, bbuf1)
        attend_last(pair, abuf0, bbuf0)
        scores_last((pair + 2) % 8, abuf0, bbuf0)
        attend_last(pair + 1, abuf1, bbuf1)

    for qc in range(2):
        at = slice(256 * qc, 256 * qc + 256)
        own = hid[2 * qc : 2 * qc + 2].reshape(256, 1024).astype(F32)
        mixed = own + dot(attn[at, :], wo[...])
        after = normalize(mixed).astype(BF)
        feat = featin[at, :] + dot(after, patt[...]) + cam_row
        both = jnp.concatenate(
            [feat[:, :128].reshape(32, 8, 128), feat[:, 128:].reshape(32, 8, 128)], axis=1
        )
        fsend[32 * qc : 32 * qc + 32] = both.astype(BF)

        @pl.loop(32 * qc, 32 * qc + 32)
        def _(m):
            @pl.when(m != mine)
            def _():
                feat_copy(m).start()

            @pl.when(m == mine)
            def _():
                pltpu.make_async_copy(fsend.at[m], frecv.at[t], feat_r).start()

    pltpu.make_async_copy(frecv, frecv, feat_r).wait()

    got = frecv[...].astype(F32)
    got = jnp.concatenate(
        [got[:, :8, :].reshape(512, 128), got[:, 8:, :].reshape(512, 128)], axis=1
    ).astype(BF)
    feat = dot(perm[...], got)
    y = normalize(feat).astype(BF)
    tq = dot(y, tqw[...]) * (LOG2E / math.sqrt(32.0))
    tkv = dot(y, tkvw[...]).astype(BF)
    same = rows((512, 128)) // 64 % 2 == lanes((512, 128)) // 64
    head = lanes((128, 128)) // 32
    ones_t = jnp.ones((128, 128), BF)
    for b in range(4):
        for g in range(2):
            at = slice(128 * b, 128 * b + 128)
            col = slice(128 * g, 128 * g + 128)
            qb = tq[at, col]
            q4 = jnp.concatenate(
                [jnp.where(head == h, qb, 0.0).astype(BF) for h in range(4)], axis=0
            )
            s = lax.dot_general(q4, tkv[at, col], NT, preferred_element_type=F32)
            s = jnp.where(same, s, -jnp.inf)
            p = jnp.exp2(s - jnp.max(s, axis=-1, keepdims=True)).astype(BF)
            v = tkv[at, 256 + 128 * g : 384 + 128 * g]
            o = dot(p, jnp.concatenate([v, ones_t], axis=1))
            num = o[:128, :128]
            den = o[:128, 128:]
            for h in range(1, 4):
                num = jnp.where(head == h, o[128 * h : 128 * h + 128, :128], num)
                den = jnp.where(head == h, o[128 * h : 128 * h + 128, 128:], den)
            tattn[at, col] = (num / den).astype(BF)
    latent = feat + dot(tattn[...], toutw[...])
    logit = jnp.sum(latent * dread_ref[...], axis=-1, keepdims=True)

    lane = lanes((64, 128))
    block = jnp.zeros((64, 128), F32)
    for p in range(8):
        block = jnp.where(lane == 8 * j + p, logit[64 * p : 64 * p + 64, :], block)
    depth = 0.1 + jnp.maximum(block, 0.0) + jnp.log(1.0 + jnp.exp(-jnp.abs(block)))
    log_depth = jnp.dot(
        spread[...], jnp.log(depth), precision=lax.Precision.HIGHEST, preferred_element_type=F32
    )

    pltpu.make_async_copy(lall, lall, lid_r).wait()
    pixel = lall[:, :8, :].reshape(256, 128).astype(jnp.int32) - (256 * block_row + 128 * c)
    hit = (pixel >= 8 * j) & (pixel < 8 * j + 8)
    predicted = jnp.take_along_axis(log_depth, jnp.clip(pixel, 0, 127), axis=1)
    error = jnp.abs(predicted - lall[:, 8:, :].reshape(256, 128))
    partial = jnp.sum(jnp.where(hit, error, 0.0))

    mixed_out = jnp.where(lane // 8 == j, depth, partial)
    for k in range(64):
        dsend[k] = mixed_out[k : k + 1, :]

    slot = 2 * (16 * (2 * block_row + c) + j)

    def depth_copy(ff, zz):
        return pltpu.make_async_remote_copy(
            src_ref=dsend.at[pl.ds(2 * ff, 2)],
            dst_ref=drecv.at[pl.ds(slot, 2)],
            send_sem=dep_s,
            recv_sem=dep_r,
            device_id=(ff, zz),
            device_id_type=MESH,
        )

    @pl.loop(0, 128)
    def _(d):
        @pl.when(d != 4 * f + z)
        def _():
            depth_copy(d // 4, d % 4).start()

        @pl.when(d == 4 * f + z)
        def _():
            pltpu.make_async_copy(
                dsend.at[pl.ds(2 * f, 2)], drecv.at[pl.ds(slot, 2)], dep_r
            ).start()

    pltpu.make_async_copy(drecv, drecv, dep_r).wait()

    group = lanes((1, 128)) // 8
    total = jnp.zeros((1, 128), F32)
    for b in range(8):
        acc = [jnp.zeros((1, 128), F32) for _ in range(2)]
        for jj in range(16):
            for i in range(2):
                part = drecv[2 * (16 * b + jj) + i]
                acc[i] = jnp.where(group == jj, part, acc[i])
                if i == 0:
                    total = total + jnp.where(group == (jj + 1) % 16, part, 0.0)
        for i in range(2):
            dfull[2 * b + i] = acc[i]
    for h in range(2):
        for i in range(2):
            depth_ref[i : i + 1, 128 * h : 128 * h + 128] = dfull[2 * (2 * z + h) + i]
    loss_ref[...] = jnp.sum(total, axis=-1, keepdims=True) * (1.0 / (8 * 64 * 512))

    pixel = lsend[:8, :].astype(jnp.int32)
    odd = rows((8, 128)) % 2 == 1
    found = jnp.ones((8, 128), F32)
    for b in range(8):
        table = jnp.where(
            odd,
            jnp.broadcast_to(dfull[2 * b + 1], (8, 128)),
            jnp.broadcast_to(dfull[2 * b], (8, 128)),
        )
        local = pixel - 128 * b
        value = jnp.take_along_axis(table, jnp.clip(local, 0, 127), axis=1)
        found = jnp.where((local >= 0) & (local < 128), value, found)
    error = jnp.where(pixel >= 0, jnp.log(found) - lsend[8:, :], 0.0)
    for k in range(4):
        perr_ref[:, 128 * k : 128 * k + 128] = error[2 * k : 2 * k + 2, :]

    for i, h in pieces:

        @pl.when(is_far(i))
        def _():
            piece_copy(i, h).wait_send()

    for piece in range(4):
        for k, buf in ((0, kbuf), (1, vbuf)):
            swap(buf, piece, k).wait_send()
    pltpu.make_async_copy(lall.at[pl.ds(0, 31)], lall.at[pl.ds(0, 31)], lid_s).wait()
    pltpu.make_async_copy(frecv.at[pl.ds(0, 63)], frecv.at[pl.ds(0, 63)], feat_s).wait()
    pltpu.make_async_copy(drecv.at[pl.ds(0, 254)], drecv.at[pl.ds(0, 254)], dep_s).wait()


def pass_on(depth_in, perr_in, loss_in, depth_out, perr_out, loss_out, sem):
    pairs = [(depth_in, depth_out), (perr_in, perr_out), (loss_in, loss_out)]
    copies = [pltpu.make_async_copy(a, b, sem.at[k]) for k, (a, b) in enumerate(pairs)]
    for copy in copies:
        copy.start()
    for copy in copies:
        copy.wait()


def body(
    hidden_in, query_weight, kv_weight, out_weight, proj_in, proj_attn, camera_table, camera_id,
    t_query, t_kv, t_out, depth_read, lidar_pixel, lidar_depth, lidar_valid,
):
    hbm = pl.BlockSpec(memory_space=pl.ANY)
    vmem = pl.BlockSpec(memory_space=pltpu.VMEM)
    smem = pl.BlockSpec(memory_space=pltpu.SMEM)
    dma = pltpu.SemaphoreType.DMA
    depth_map, point_error, loss = pl.pallas_call(
        kernel,
        out_shape=(
            jax.ShapeDtypeStruct((2, 256), F32),
            jax.ShapeDtypeStruct((2, 512), F32),
            jax.ShapeDtypeStruct((1, 1), F32),
        ),
        in_specs=[
            hbm, hbm, hbm, hbm, hbm, hbm, vmem, smem, hbm, hbm, hbm, vmem, vmem, vmem, vmem,
        ],
        out_specs=(vmem, vmem, vmem),
        scratch_shapes=[
            pltpu.VMEM((4, 128, 1024), BF),
            pltpu.VMEM((1024, 1024), BF),
            pltpu.VMEM((1024, 2048), BF),
            pltpu.VMEM((1024, 1024), BF),
            pltpu.VMEM((1024, 256), BF),
            pltpu.VMEM((1024, 256), BF),
            pltpu.VMEM((256, 256), BF),
            pltpu.VMEM((256, 512), BF),
            pltpu.VMEM((256, 256), BF),
            pltpu.VMEM((512, 1024), BF),
            pltpu.VMEM((2, 512, 1024), BF),
            pltpu.VMEM((1024, 1024), BF),
            pltpu.VMEM((1024, 1024), BF),
            pltpu.VMEM((768, 768), F32),
            pltpu.VMEM((768, 768), F32),
            pltpu.VMEM((768, 256), F32),
            pltpu.VMEM((768, 256), F32),
            pltpu.VMEM((256, 1024), F32),
            pltpu.VMEM((256, 1024), F32),
            pltpu.VMEM((8, 768, 256), F32),
            pltpu.VMEM((8, 768, 128), F32),
            pltpu.VMEM((512, 1024), BF),
            pltpu.VMEM((512, 256), F32),
            pltpu.VMEM((64, 16, 128), BF),
            pltpu.VMEM((64, 16, 128), BF),
            pltpu.VMEM((512, 512), BF),
            pltpu.VMEM((256, 64), F32),
            pltpu.VMEM((512, 256), BF),
            pltpu.VMEM((16, 128), F32),
            pltpu.VMEM((32, 16, 128), F32),
            pltpu.VMEM((64, 1, 128), F32),
            pltpu.VMEM((256, 1, 128), F32),
            pltpu.VMEM((16, 1, 128), F32),
            pltpu.SemaphoreType.REGULAR, pltpu.SemaphoreType.REGULAR,
            dma((8,)), dma((4,)), dma((4,)), dma((2, 4)), dma((2, 4)),
            dma, dma, dma, dma, dma, dma,
        ],
        compiler_params=pltpu.CompilerParams(
            collective_id=0, has_side_effects=True, vmem_limit_bytes=56 * 2**20
        ),
        cost_estimate=pl.CostEstimate(
            flops=8_000_000_000, bytes_accessed=12_000_000, transcendentals=9_000_000
        ),
    )(
        hidden_in, query_weight, kv_weight, out_weight, proj_in, proj_attn, camera_table,
        camera_id, t_query, t_kv, t_out, depth_read.reshape(1, -1), lidar_pixel, lidar_depth,
        lidar_valid,
    )
    depth_map, point_error, loss = pl.pallas_call(
        pass_on,
        out_shape=(
            jax.ShapeDtypeStruct((2, 256), F32),
            jax.ShapeDtypeStruct((2, 512), F32),
            jax.ShapeDtypeStruct((1, 1), F32),
        ),
        in_specs=[hbm, hbm, hbm],
        out_specs=(hbm, hbm, hbm),
        scratch_shapes=[dma((3,))],
    )(depth_map, point_error, loss)
    return depth_map, point_error, loss.reshape(())


def solution(mesh):
    return jax.shard_map(
        body,
        mesh=mesh,
        in_specs=(
            P("frame", "row", None),
            P(),
            P(),
            P(),
            P(),
            P(),
            P(),
            P(),
            P(),
            P(),
            P(),
            P(),
            P("frame", None),
            P("frame", None),
            P("frame", None),
        ),
        out_specs=(P("frame", "row"), P("frame", None), P()),
        check_vma=False,
    )
```

```python
import functools
import math

import jax
import jax.numpy as jnp
from jax import lax
from jax.experimental import pallas as pl
from jax.experimental.pallas import tpu as pltpu
from jax.sharding import PartitionSpec as P

MESH = pl.DeviceIdType.MESH
BF = jnp.bfloat16
F32 = jnp.float32
LOG2E = 1.4426950408889634
T_HEADS = 8
CAMERAS = 6
NT = (((1,), (1,)), ((), ()))


def normalize(values):
    mean = jnp.mean(values, axis=-1, keepdims=True)
    centred = values - mean
    var = jnp.mean(centred * centred, axis=-1, keepdims=True)
    return centred * lax.rsqrt(var + 1e-06)


def dot(a, b):
    return jnp.dot(a, b, preferred_element_type=F32)


def lanes(shape):
    return lax.broadcasted_iota(jnp.int32, shape, len(shape) - 1)


def rows(shape):
    return lax.broadcasted_iota(jnp.int32, shape, len(shape) - 2)


def kernel(
    x_ref, wq_h, wkv_h, wo_h, pin_h, patt_h, cam_ref, cid_ref, tq_h, tkv_h, tout_h, dread_ref,
    lpix_ref, ldep_ref, lval_ref,
    depth_ref, perr_ref, loss_ref,
    hid, wq, wkv, wo, pin, patt, tqw, tkvw, toutw,
    normed, qm, ktbuf, vbuf, sbuf0, sbuf1, abuf0, abuf1, bbuf0, bbuf1, obuf, mbuf, attn, featin, fsend, frecv,
    perm, spread, tattn, lsend, lall, dsend, drecv, dfull,
    here_x, here_y, wsem, hid_s, hid_r, kv_s, kv_r, lid_s, lid_r, feat_s, feat_r, dep_s, dep_r,
):
    f = lax.axis_index("frame")
    z = lax.axis_index("row")
    j = f // 2
    c = f % 2
    t = 4 * j + z

    barrier = pltpu.get_barrier_semaphore()

    gx, gy = f // 8, j % 4
    column = [(2 * j + (c + dc) % 2, (z + dz) % 4) for dz in range(4) for dc in range(2)][1:]
    along_x = [(8 * ((gx + d) % 4) + 2 * gy + c, z) for d in range(1, 4)]
    along_y = [(8 * gx + 2 * ((gy + d) % 4) + c, z) for d in range(1, 4)]
    for device in column + along_x + along_y:
        pl.semaphore_signal(barrier, inc=1, device_id=device, device_id_type=MESH)

    weights = [
        pltpu.make_async_copy(src, dst, wsem.at[k])
        for k, (src, dst) in enumerate(
            [(wkv_h, wkv), (wq_h, wq), (pin_h, pin), (wo_h, wo), (patt_h, patt),
             (tq_h, tqw), (tkv_h, tkvw), (tout_h, toutw)]
        )
    ]
    for copy in weights:
        copy.start()

    for k in range(4):
        part = slice(128 * k, 128 * k + 128)
        pixel = jnp.where(lval_ref[:, part] != 0, lpix_ref[:, part], -1).astype(F32)
        lsend[2 * k : 2 * k + 2, :] = pixel
        lsend[8 + 2 * k : 10 + 2 * k, :] = jnp.log(ldep_ref[:, part])
    own_points = pltpu.make_async_copy(lsend, lall.at[f], lid_r)
    own_points.start()

    pl.semaphore_wait(barrier, 13)

    def slot_of(i):
        far = (z - 2 * c - i + 4) % 4
        return jnp.where(far == 2, 3, jnp.where(far == 3, 2, far))

    def piece_copy(i, h):
        return pltpu.make_async_remote_copy(
            src_ref=x_ref.at[i, pl.ds(128 * h, 128)],
            dst_ref=hid.at[slot_of(i)],
            send_sem=hid_s.at[2 * i + h],
            recv_sem=hid_r.at[slot_of(i)],
            device_id=(2 * j + h, 2 * c + i),
            device_id_type=MESH,
        )

    def piece_here(i, h):
        return (2 * c + i == z) & (h == c)

    pieces = [(i, h) for i in range(2) for h in range(2)]

    def is_far(i):
        return (2 * c + i - z + 4) % 4 == 2

    for i, h in pieces:

        @pl.when(jnp.logical_not(piece_here(i, h) | is_far(i)))
        def _():
            piece_copy(i, h).start()

    for i, h in pieces:

        @pl.when(piece_here(i, h))
        def _():
            pltpu.make_async_copy(
                x_ref.at[i, pl.ds(128 * h, 128)], hid.at[0], hid_r.at[0]
            ).start()

    for device in along_x:
        pl.semaphore_signal(here_x, inc=1, device_id=device, device_id_type=MESH)

    row = rows((512, 512))
    perm[...] = jnp.where(lanes((512, 512)) == (row % 64) * 8 + row // 64, 1.0, 0.0).astype(BF)
    row = rows((256, 64))
    spread[...] = jnp.where(lanes((256, 64)) == 2 * (row // 8) + row % 2, 1.0, 0.0)

    pl.semaphore_wait(here_x, 3)
    for device in along_y:
        pl.semaphore_signal(here_y, inc=1, device_id=device, device_id_type=MESH)

    def swap_keys(piece):
        return pltpu.make_async_remote_copy(
            src_ref=ktbuf.at[2 * piece],
            dst_ref=ktbuf.at[2 * piece + 1],
            send_sem=kv_s.at[0, piece],
            recv_sem=kv_r.at[0, piece],
            device_id=(2 * j + 1 - c, z),
            device_id_type=MESH,
        )

    def swap_values(piece):
        return pltpu.make_async_remote_copy(
            src_ref=vbuf.at[pl.ds(256 * piece, 128)],
            dst_ref=vbuf.at[pl.ds(256 * piece + 128, 128)],
            send_sem=kv_s.at[1, piece],
            recv_sem=kv_r.at[1, piece],
            device_id=(2 * j + 1 - c, z),
            device_id_type=MESH,
        )

    for copy in weights[:3]:
        copy.wait()

    def points_copy(ff):
        return pltpu.make_async_remote_copy(
            src_ref=lsend,
            dst_ref=lall.at[f],
            send_sem=lid_s,
            recv_sem=lid_r,
            device_id=(ff, z),
            device_id_type=MESH,
        )

    def project(first, count):
        for piece in range(first, first + count):
            pltpu.make_async_copy(hid.at[piece], hid.at[piece], hid_r.at[piece]).wait()
        size = 128 * count
        at = slice(128 * first, 128 * first + size)
        own = hid[first : first + count].reshape(size, 1024)
        normed[at, :] = normalize(own.astype(F32)).astype(BF)
        key = dot(normed[at, :], wkv[:, :1024]).astype(BF)
        for k in range(count):
            ktbuf[2 * (first + k)] = key[128 * k : 128 * k + 128].T
            swap_keys(first + k).start()
        value = dot(normed[at, :], wkv[:, 1024:]).astype(BF)
        for k in range(count):
            row = 256 * (first + k)
            vbuf[row : row + 128, :] = value[128 * k : 128 * k + 128]
            swap_values(first + k).start()
        q = dot(normed[at, :], wq[...]) * (LOG2E / 8.0)
        low = lanes((size, 1024)) % 128 < 64
        qm[0, at, :] = jnp.where(low, q, 0.0).astype(BF)
        qm[1, at, :] = jnp.where(low, 0.0, q).astype(BF)
        featin[at, :] = dot(normed[at, :], pin[...])

    project(0, 1)
    pl.semaphore_wait(here_y, 3)

    @pl.loop(1, 32)
    def _(ff):
        points_copy((f + ff) % 32).start()

    for i, h in pieces:

        @pl.when(jnp.logical_not(piece_here(i, h) | is_far(i)))
        def _():
            piece_copy(i, h).wait_send()

    for i, h in pieces:

        @pl.when(is_far(i))
        def _():
            piece_copy(i, h).start()

    project(1, 2)

    camera = cid_ref[t]
    cam_row = jnp.zeros((1, 256), F32)
    for k in range(CAMERAS):
        cam_row = cam_row + cam_ref[k : k + 1, :].astype(F32) * jnp.where(camera == k, 1.0, 0.0)

    for piece in range(3):
        swap_keys(piece).wait_recv()
        swap_values(piece).wait_recv()
    for copy in weights[3:]:
        copy.wait()

    def keys_of(first, last, col):
        return jnp.concatenate([ktbuf[k, col, :] for k in range(first, last)], axis=1)

    def scores_first(pair, out):
        col = pl.ds(pl.multiple_of(128 * pair, 128), 128)
        q2 = qm[:, :384, col].reshape(768, 128)
        out[...] = dot(q2, keys_of(0, 6, col))

    def values(at, col, count):
        return jnp.concatenate([vbuf[at, col], jnp.ones((count, 128), BF)], axis=1)

    def attend_first(pair, s_ref):
        col = pl.ds(pl.multiple_of(128 * pair, 128), 128)
        s = s_ref[...]
        top = jnp.max(s, axis=-1, keepdims=True)
        p = jnp.exp2((s - top).astype(BF))
        obuf[pair] = dot(p, values(slice(0, 768), col, 768))
        mbuf[pair] = jnp.broadcast_to(top, (768, 128))

    def scores_last(pair, out_a, out_b):
        col = pl.ds(pl.multiple_of(128 * pair, 128), 128)
        q2 = qm[:, :384, col].reshape(768, 128)
        out_a[...] = dot(q2, keys_of(6, 8, col))
        q2 = qm[:, 384:, col].reshape(256, 128)
        out_b[...] = dot(q2, keys_of(0, 8, col))

    def heads_of(o, count):
        left = lanes((count, 128)) < 64
        num = jnp.where(left, o[:count, :128], o[count:, :128])
        den = jnp.where(left, o[:count, 128:], o[count:, 128:])
        return (num / den).astype(BF)

    def attend_last(pair, a_ref, b_ref):
        col = pl.ds(pl.multiple_of(128 * pair, 128), 128)
        s = a_ref[...]
        before = mbuf[pair]
        top = jnp.maximum(before, jnp.max(s, axis=-1, keepdims=True))
        p = jnp.exp2((s - jnp.concatenate([top, top], axis=1)).astype(BF))
        keep = jnp.exp2(before - top)
        o = obuf[pair] * jnp.concatenate([keep, keep], axis=1)
        o = o + dot(p, values(slice(768, 1024), col, 256))
        attn[:384, col] = heads_of(o, 384)
        s = b_ref[...]
        p = jnp.exp2((s - jnp.max(s, axis=-1, keepdims=True)).astype(BF))
        attn[384:, col] = heads_of(dot(p, values(slice(0, 1024), col, 1024)), 128)

    def row_of(piece):
        return (z + 2 + (0, 1, 3, 2)[piece]) % 4

    offsets = [(dx, dy) for dx in range(4) for dy in range(4)]
    offsets.sort(key=lambda o: min(o[0], 4 - o[0]) + min(o[1], 4 - o[1]))

    def feat_copy(piece, dx, dy):
        other = 4 * ((gx + dx) % 4) + (gy + dy) % 4
        return pltpu.make_async_remote_copy(
            src_ref=fsend.at[16 * piece + other],
            dst_ref=frecv.at[t],
            send_sem=feat_s,
            recv_sem=feat_r,
            device_id=(2 * other + c, row_of(piece)),
            device_id_type=MESH,
        )

    block_row = (z + 2) % 4
    scores_first(0, sbuf0)

    @pl.loop(0, 4)
    def _(step):
        @pl.when(step == 3)
        def _():
            project(3, 1)

        pair = 2 * step
        scores_first(pair + 1, sbuf1)
        attend_first(pair, sbuf0)
        scores_first((pair + 2) % 8, sbuf0)
        attend_first(pair + 1, sbuf1)

    swap_keys(3).wait_recv()
    swap_values(3).wait_recv()
    scores_last(0, abuf0, bbuf0)

    @pl.loop(0, 4)
    def _(step):
        pair = 2 * step
        scores_last(pair + 1, abuf1, bbuf1)
        attend_last(pair, abuf0, bbuf0)
        scores_last((pair + 2) % 8, abuf0, bbuf0)
        attend_last(pair + 1, abuf1, bbuf1)

    for piece in range(4):
        at = slice(128 * piece, 128 * piece + 128)
        mixed = hid[piece].astype(F32) + dot(attn[at, :], wo[...])
        after = normalize(mixed).astype(BF)
        feat = featin[at, :] + dot(after, patt[...]) + cam_row
        both = jnp.concatenate(
            [feat[:, :128].reshape(16, 8, 128), feat[:, 128:].reshape(16, 8, 128)], axis=1
        )
        fsend[16 * piece : 16 * piece + 16] = both.astype(BF)
        for dx, dy in reversed(offsets[int(piece == 3) :]):
            feat_copy(piece, dx, dy).start()
    pltpu.make_async_copy(fsend.at[48 + j], frecv.at[t], feat_r).start()

    pltpu.make_async_copy(frecv, frecv, feat_r).wait()

    got = frecv[...].astype(F32)
    got = jnp.concatenate(
        [got[:, :8, :].reshape(512, 128), got[:, 8:, :].reshape(512, 128)], axis=1
    ).astype(BF)
    feat = dot(perm[...], got)
    y = normalize(feat).astype(BF)
    tq = dot(y, tqw[...]) * (LOG2E / math.sqrt(32.0))
    tkv = dot(y, tkvw[...]).astype(BF)
    same = rows((512, 128)) // 64 % 2 == lanes((512, 128)) // 64
    head = lanes((128, 128)) // 32
    ones_t = jnp.ones((128, 128), BF)
    for b in range(4):
        for g in range(2):
            at = slice(128 * b, 128 * b + 128)
            col = slice(128 * g, 128 * g + 128)
            qb = tq[at, col]
            q4 = jnp.concatenate(
                [jnp.where(head == h, qb, 0.0).astype(BF) for h in range(4)], axis=0
            )
            s = lax.dot_general(q4, tkv[at, col], NT, preferred_element_type=F32)
            s = jnp.where(same, s, -jnp.inf)
            p = jnp.exp2(s - jnp.max(s, axis=-1, keepdims=True)).astype(BF)
            v = tkv[at, 256 + 128 * g : 384 + 128 * g]
            o = dot(p, jnp.concatenate([v, ones_t], axis=1))
            num = o[:128, :128]
            den = o[:128, 128:]
            for h in range(1, 4):
                num = jnp.where(head == h, o[128 * h : 128 * h + 128, :128], num)
                den = jnp.where(head == h, o[128 * h : 128 * h + 128, 128:], den)
            tattn[at, col] = (num / den).astype(BF)
    latent = feat + dot(tattn[...], toutw[...])
    logit = jnp.sum(latent * dread_ref[...], axis=-1, keepdims=True)

    lane = lanes((64, 128))
    block = jnp.zeros((64, 128), F32)
    for p in range(8):
        block = jnp.where(lane == 8 * j + p, logit[64 * p : 64 * p + 64, :], block)
    depth = 0.1 + jnp.maximum(block, 0.0) + jnp.log(1.0 + jnp.exp(-jnp.abs(block)))
    log_depth = jnp.dot(
        spread[...], jnp.log(depth), precision=lax.Precision.HIGHEST, preferred_element_type=F32
    )

    pltpu.make_async_copy(lall, lall, lid_r).wait()
    pixel = lall[:, :8, :].reshape(256, 128).astype(jnp.int32) - (256 * block_row + 128 * c)
    hit = (pixel >= 8 * j) & (pixel < 8 * j + 8)
    predicted = jnp.take_along_axis(log_depth, jnp.clip(pixel, 0, 127), axis=1)
    error = jnp.abs(predicted - lall[:, 8:, :].reshape(256, 128))
    partial = jnp.sum(jnp.where(hit, error, 0.0))

    mixed_out = jnp.where(lane // 8 == j, depth, partial)
    for k in range(64):
        dsend[k] = mixed_out[k : k + 1, :]

    slot = 2 * (16 * (2 * block_row + c) + j)

    def depth_copy(ff, zz):
        return pltpu.make_async_remote_copy(
            src_ref=dsend.at[pl.ds(2 * ff, 2)],
            dst_ref=drecv.at[pl.ds(slot, 2)],
            send_sem=dep_s,
            recv_sem=dep_r,
            device_id=(ff, zz),
            device_id_type=MESH,
        )

    def hops(offset):
        return sum(min(d, 4 - d) for d in offset[:3])

    everyone = [
        (dx, dy, dz, dc)
        for dx in range(4) for dy in range(4) for dz in range(4) for dc in range(2)
    ][1:]
    for dx, dy, dz, dc in sorted(everyone, key=hops, reverse=True):
        depth_copy(
            8 * ((gx + dx) % 4) + 2 * ((gy + dy) % 4) + (c + dc) % 2, (z + dz) % 4
        ).start()
    pltpu.make_async_copy(dsend.at[pl.ds(2 * f, 2)], drecv.at[pl.ds(slot, 2)], dep_r).start()

    pltpu.make_async_copy(drecv, drecv, dep_r).wait()

    group = lanes((1, 128)) // 8
    total = jnp.zeros((1, 128), F32)
    for b in range(8):
        acc = [jnp.zeros((1, 128), F32) for _ in range(2)]
        for jj in range(16):
            for i in range(2):
                part = drecv[2 * (16 * b + jj) + i]
                acc[i] = jnp.where(group == jj, part, acc[i])
                if i == 0:
                    total = total + jnp.where(group == (jj + 1) % 16, part, 0.0)
        for i in range(2):
            dfull[2 * b + i] = acc[i]
    for h in range(2):
        for i in range(2):
            depth_ref[i : i + 1, 128 * h : 128 * h + 128] = dfull[2 * (2 * z + h) + i]
    loss_ref[...] = jnp.sum(total, axis=-1, keepdims=True) * (1.0 / (8 * 64 * 512))

    pixel = lsend[:8, :].astype(jnp.int32)
    odd = rows((8, 128)) % 2 == 1
    found = jnp.ones((8, 128), F32)
    for b in range(8):
        table = jnp.where(
            odd,
            jnp.broadcast_to(dfull[2 * b + 1], (8, 128)),
            jnp.broadcast_to(dfull[2 * b], (8, 128)),
        )
        local = pixel - 128 * b
        value = jnp.take_along_axis(table, jnp.clip(local, 0, 127), axis=1)
        found = jnp.where((local >= 0) & (local < 128), value, found)
    error = jnp.where(pixel >= 0, jnp.log(found) - lsend[8:, :], 0.0)
    for k in range(4):
        perr_ref[:, 128 * k : 128 * k + 128] = error[2 * k : 2 * k + 2, :]

    for i, h in pieces:

        @pl.when(is_far(i))
        def _():
            piece_copy(i, h).wait_send()

    for piece in range(4):
        swap_keys(piece).wait_send()
        swap_values(piece).wait_send()
    pltpu.make_async_copy(lall.at[pl.ds(0, 31)], lall.at[pl.ds(0, 31)], lid_s).wait()
    pltpu.make_async_copy(frecv.at[pl.ds(0, 63)], frecv.at[pl.ds(0, 63)], feat_s).wait()
    pltpu.make_async_copy(drecv.at[pl.ds(0, 254)], drecv.at[pl.ds(0, 254)], dep_s).wait()


def pass_on(depth_in, perr_in, loss_in, depth_out, perr_out, loss_out, sem):
    pairs = [(depth_in, depth_out), (perr_in, perr_out), (loss_in, loss_out)]
    copies = [pltpu.make_async_copy(a, b, sem.at[k]) for k, (a, b) in enumerate(pairs)]
    for copy in copies:
        copy.start()
    for copy in copies:
        copy.wait()


def body(
    hidden_in, query_weight, kv_weight, out_weight, proj_in, proj_attn, camera_table, camera_id,
    t_query, t_kv, t_out, depth_read, lidar_pixel, lidar_depth, lidar_valid,
):
    hbm = pl.BlockSpec(memory_space=pl.ANY)
    vmem = pl.BlockSpec(memory_space=pltpu.VMEM)
    smem = pl.BlockSpec(memory_space=pltpu.SMEM)
    dma = pltpu.SemaphoreType.DMA
    depth_map, point_error, loss = pl.pallas_call(
        kernel,
        out_shape=(
            jax.ShapeDtypeStruct((2, 256), F32),
            jax.ShapeDtypeStruct((2, 512), F32),
            jax.ShapeDtypeStruct((1, 1), F32),
        ),
        in_specs=[
            hbm, hbm, hbm, hbm, hbm, hbm, vmem, smem, hbm, hbm, hbm, vmem, vmem, vmem, vmem,
        ],
        out_specs=(vmem, vmem, vmem),
        scratch_shapes=[
            pltpu.VMEM((4, 128, 1024), BF),
            pltpu.VMEM((1024, 1024), BF),
            pltpu.VMEM((1024, 2048), BF),
            pltpu.VMEM((1024, 1024), BF),
            pltpu.VMEM((1024, 256), BF),
            pltpu.VMEM((1024, 256), BF),
            pltpu.VMEM((256, 256), BF),
            pltpu.VMEM((256, 512), BF),
            pltpu.VMEM((256, 256), BF),
            pltpu.VMEM((512, 1024), BF),
            pltpu.VMEM((2, 512, 1024), BF),
            pltpu.VMEM((8, 1024, 128), BF),
            pltpu.VMEM((1024, 1024), BF),
            pltpu.VMEM((768, 768), F32),
            pltpu.VMEM((768, 768), F32),
            pltpu.VMEM((768, 256), F32),
            pltpu.VMEM((768, 256), F32),
            pltpu.VMEM((256, 1024), F32),
            pltpu.VMEM((256, 1024), F32),
            pltpu.VMEM((8, 768, 256), F32),
            pltpu.VMEM((8, 768, 128), F32),
            pltpu.VMEM((512, 1024), BF),
            pltpu.VMEM((512, 256), F32),
            pltpu.VMEM((64, 16, 128), BF),
            pltpu.VMEM((64, 16, 128), BF),
            pltpu.VMEM((512, 512), BF),
            pltpu.VMEM((256, 64), F32),
            pltpu.VMEM((512, 256), BF),
            pltpu.VMEM((16, 128), F32),
            pltpu.VMEM((32, 16, 128), F32),
            pltpu.VMEM((64, 1, 128), F32),
            pltpu.VMEM((256, 1, 128), F32),
            pltpu.VMEM((16, 1, 128), F32),
            pltpu.SemaphoreType.REGULAR, pltpu.SemaphoreType.REGULAR,
            dma((8,)), dma((4,)), dma((4,)), dma((2, 4)), dma((2, 4)),
            dma, dma, dma, dma, dma, dma,
        ],
        compiler_params=pltpu.CompilerParams(
            collective_id=0, has_side_effects=True, vmem_limit_bytes=56 * 2**20
        ),
        cost_estimate=pl.CostEstimate(
            flops=8_000_000_000, bytes_accessed=12_000_000, transcendentals=9_000_000
        ),
    )(
        hidden_in, query_weight, kv_weight, out_weight, proj_in, proj_attn, camera_table,
        camera_id, t_query, t_kv, t_out, depth_read.reshape(1, -1), lidar_pixel, lidar_depth,
        lidar_valid,
    )
    depth_map, point_error, loss = pl.pallas_call(
        pass_on,
        out_shape=(
            jax.ShapeDtypeStruct((2, 256), F32),
            jax.ShapeDtypeStruct((2, 512), F32),
            jax.ShapeDtypeStruct((1, 1), F32),
        ),
        in_specs=[hbm, hbm, hbm],
        out_specs=(hbm, hbm, hbm),
        scratch_shapes=[dma((3,))],
    )(depth_map, point_error, loss)
    return depth_map, point_error, loss.reshape(())


def solution(mesh):
    return jax.shard_map(
        body,
        mesh=mesh,
        in_specs=(
            P("frame", "row", None),
            P(),
            P(),
            P(),
            P(),
            P(),
            P(),
            P(),
            P(),
            P(),
            P(),
            P(),
            P("frame", None),
            P("frame", None),
            P("frame", None),
        ),
        out_specs=(P("frame", "row"), P("frame", None), P()),
        check_vma=False,
    )
```

```python
import functools
import math

import jax
import jax.numpy as jnp
from jax import lax
from jax.experimental import pallas as pl
from jax.experimental.pallas import tpu as pltpu
from jax.sharding import PartitionSpec as P

MESH = pl.DeviceIdType.MESH
BF = jnp.bfloat16
F32 = jnp.float32
LOG2E = 1.4426950408889634
T_HEADS = 8
CAMERAS = 6
NT = (((1,), (1,)), ((), ()))


def normalize(values):
    mean = jnp.mean(values, axis=-1, keepdims=True)
    centred = values - mean
    var = jnp.mean(centred * centred, axis=-1, keepdims=True)
    return centred * lax.rsqrt(var + 1e-06)


def dot(a, b):
    return jnp.dot(a, b, preferred_element_type=F32)


def lanes(shape):
    return lax.broadcasted_iota(jnp.int32, shape, len(shape) - 1)


def rows(shape):
    return lax.broadcasted_iota(jnp.int32, shape, len(shape) - 2)


def kernel(
    x_ref, wq_h, wkv_h, wo_h, pin_h, patt_h, cam_ref, cid_ref, tq_h, tkv_h, tout_h, dread_ref,
    lpix_ref, ldep_ref, lval_ref,
    depth_ref, perr_ref, loss_ref,
    hid, wq, wkv, wo, pin, patt, tqw, tkvw, toutw,
    normed, qm, ktbuf, vbuf, sbuf0, sbuf1, abuf0, abuf1, bbuf0, bbuf1, obuf, mbuf, attn, featin, fsend, frecv,
    perm, spread, tattn, lsend, lall, dsend, drecv, dfull,
    here_x, here_y, wsem, hid_s, hid_r, kv_s, kv_r, lid_s, lid_r, feat_s, feat_r, dep_s, dep_r,
):
    f = lax.axis_index("frame")
    z = lax.axis_index("row")
    j = f // 2
    c = f % 2
    t = 4 * j + z

    barrier = pltpu.get_barrier_semaphore()

    gx, gy = f // 8, j % 4
    column = [(2 * j + (c + dc) % 2, (z + dz) % 4) for dz in range(4) for dc in range(2)][1:]
    along_x = [(8 * ((gx + d) % 4) + 2 * gy + c, z) for d in range(1, 4)]
    along_y = [(8 * gx + 2 * ((gy + d) % 4) + c, z) for d in range(1, 4)]
    for device in column + along_x + along_y:
        pl.semaphore_signal(barrier, inc=1, device_id=device, device_id_type=MESH)

    weights = [
        pltpu.make_async_copy(src, dst, wsem.at[k])
        for k, (src, dst) in enumerate(
            [(wkv_h, wkv), (wq_h, wq), (pin_h, pin), (wo_h, wo), (patt_h, patt),
             (tq_h, tqw), (tkv_h, tkvw), (tout_h, toutw)]
        )
    ]
    for copy in weights:
        copy.start()

    for k in range(4):
        part = slice(128 * k, 128 * k + 128)
        pixel = jnp.where(lval_ref[:, part] != 0, lpix_ref[:, part], -1).astype(F32)
        lsend[2 * k : 2 * k + 2, :] = pixel
        lsend[8 + 2 * k : 10 + 2 * k, :] = jnp.log(ldep_ref[:, part])
    own_points = pltpu.make_async_copy(lsend, lall.at[f], lid_r)
    own_points.start()

    pl.semaphore_wait(barrier, 13)

    def slot_of(i):
        far = (z - 2 * c - i + 4) % 4
        return jnp.where(far == 2, 3, jnp.where(far == 3, 2, far))

    def piece_copy(i, h):
        return pltpu.make_async_remote_copy(
            src_ref=x_ref.at[i, pl.ds(128 * h, 128)],
            dst_ref=hid.at[slot_of(i)],
            send_sem=hid_s.at[2 * i + h],
            recv_sem=hid_r.at[slot_of(i)],
            device_id=(2 * j + h, 2 * c + i),
            device_id_type=MESH,
        )

    def piece_here(i, h):
        return (2 * c + i == z) & (h == c)

    pieces = [(i, h) for i in range(2) for h in range(2)]

    def is_far(i):
        return (2 * c + i - z + 4) % 4 == 2

    for i, h in pieces:

        @pl.when(jnp.logical_not(piece_here(i, h) | is_far(i)))
        def _():
            piece_copy(i, h).start()

    for i, h in pieces:

        @pl.when(piece_here(i, h))
        def _():
            pltpu.make_async_copy(
                x_ref.at[i, pl.ds(128 * h, 128)], hid.at[0], hid_r.at[0]
            ).start()

    for device in along_x:
        pl.semaphore_signal(here_x, inc=1, device_id=device, device_id_type=MESH)

    row = rows((512, 512))
    perm[...] = jnp.where(lanes((512, 512)) == (row % 64) * 8 + row // 64, 1.0, 0.0).astype(BF)
    row = rows((256, 64))
    spread[...] = jnp.where(lanes((256, 64)) == 2 * (row // 8) + row % 2, 1.0, 0.0)

    pl.semaphore_wait(here_x, 3)
    for device in along_y:
        pl.semaphore_signal(here_y, inc=1, device_id=device, device_id_type=MESH)

    def swap_keys(piece):
        return pltpu.make_async_remote_copy(
            src_ref=ktbuf.at[2 * piece],
            dst_ref=ktbuf.at[2 * piece + 1],
            send_sem=kv_s.at[0, piece],
            recv_sem=kv_r.at[0, piece],
            device_id=(2 * j + 1 - c, z),
            device_id_type=MESH,
        )

    def swap_values(piece):
        return pltpu.make_async_remote_copy(
            src_ref=vbuf.at[pl.ds(256 * piece, 128)],
            dst_ref=vbuf.at[pl.ds(256 * piece + 128, 128)],
            send_sem=kv_s.at[1, piece],
            recv_sem=kv_r.at[1, piece],
            device_id=(2 * j + 1 - c, z),
            device_id_type=MESH,
        )

    for copy in weights[:3]:
        copy.wait()

    def points_copy(ff):
        return pltpu.make_async_remote_copy(
            src_ref=lsend,
            dst_ref=lall.at[f],
            send_sem=lid_s,
            recv_sem=lid_r,
            device_id=(ff, z),
            device_id_type=MESH,
        )

    def project(first, count):
        for piece in range(first, first + count):
            pltpu.make_async_copy(hid.at[piece], hid.at[piece], hid_r.at[piece]).wait()
        size = 128 * count
        at = slice(128 * first, 128 * first + size)
        own = hid[first : first + count].reshape(size, 1024)
        normed[at, :] = normalize(own.astype(F32)).astype(BF)
        key = dot(normed[at, :], wkv[:, :1024]).astype(BF)
        for k in range(count):
            ktbuf[2 * (first + k)] = key[128 * k : 128 * k + 128].T
            swap_keys(first + k).start()
        value = dot(normed[at, :], wkv[:, 1024:]).astype(BF)
        for k in range(count):
            row = 256 * (first + k)
            vbuf[row : row + 128, :] = value[128 * k : 128 * k + 128]
            swap_values(first + k).start()
        q = dot(normed[at, :], wq[...]) * (LOG2E / 8.0)
        low = lanes((size, 1024)) % 128 < 64
        qm[0, at, :] = jnp.where(low, q, 0.0).astype(BF)
        qm[1, at, :] = jnp.where(low, 0.0, q).astype(BF)
        featin[at, :] = dot(normed[at, :], pin[...])

    project(0, 1)
    pl.semaphore_wait(here_y, 3)

    @pl.loop(1, 32)
    def _(ff):
        points_copy((f + ff) % 32).start()

    for i, h in pieces:

        @pl.when(jnp.logical_not(piece_here(i, h) | is_far(i)))
        def _():
            piece_copy(i, h).wait_send()

    for i, h in pieces:

        @pl.when(is_far(i))
        def _():
            piece_copy(i, h).start()

    project(1, 2)

    camera = cid_ref[t]
    cam_row = jnp.zeros((1, 256), F32)
    for k in range(CAMERAS):
        cam_row = cam_row + cam_ref[k : k + 1, :].astype(F32) * jnp.where(camera == k, 1.0, 0.0)

    for piece in range(3):
        swap_keys(piece).wait_recv()
        swap_values(piece).wait_recv()
    for copy in weights[3:]:
        copy.wait()

    def at_pair(pair):
        return pl.ds(128 * pair if isinstance(pair, int) else pl.multiple_of(128 * pair, 128), 128)

    def keys_of(first, last, col):
        return jnp.concatenate([ktbuf[k, col, :] for k in range(first, last)], axis=1)

    def scores_first(pair, out):
        col = at_pair(pair)
        q2 = qm[:, :384, col].reshape(768, 128)
        out[...] = dot(q2, keys_of(0, 6, col))

    def values(at, col, count):
        return jnp.concatenate([vbuf[at, col], jnp.ones((count, 128), BF)], axis=1)

    def attend_first(pair, s_ref):
        col = at_pair(pair)
        s = s_ref[...]
        top = jnp.max(s, axis=-1, keepdims=True)
        p = jnp.exp2((s - top).astype(BF))
        obuf[pair] = dot(p, values(slice(0, 768), col, 768))
        mbuf[pair] = jnp.broadcast_to(top, (768, 128))

    def scores_merge(pair, out):
        col = at_pair(pair)
        q2 = qm[:, :384, col].reshape(768, 128)
        out[...] = dot(q2, keys_of(6, 8, col))

    def scores_last(pair, out):
        col = at_pair(pair)
        q2 = qm[:, 384:, col].reshape(256, 128)
        out[...] = dot(q2, keys_of(0, 8, col))

    def heads_of(o, count):
        left = lanes((count, 128)) < 64
        num = jnp.where(left, o[:count, :128], o[count:, :128])
        den = jnp.where(left, o[:count, 128:], o[count:, 128:])
        return (num / den).astype(BF)

    def attend_merge(pair, s_ref):
        col = at_pair(pair)
        s = s_ref[...]
        before = mbuf[pair]
        top = jnp.maximum(before, jnp.max(s, axis=-1, keepdims=True))
        p = jnp.exp2((s - jnp.concatenate([top, top], axis=1)).astype(BF))
        keep = jnp.exp2(before - top)
        o = obuf[pair] * jnp.concatenate([keep, keep], axis=1)
        o = o + dot(p, values(slice(768, 1024), col, 256))
        attn[:384, col] = heads_of(o, 384)

    def attend_last(pair, s_ref):
        col = at_pair(pair)
        s = s_ref[...]
        p = jnp.exp2((s - jnp.max(s, axis=-1, keepdims=True)).astype(BF))
        attn[384:, col] = heads_of(dot(p, values(slice(0, 1024), col, 1024)), 128)

    def row_of(piece):
        return (z + 2 + (0, 1, 3, 2)[piece]) % 4

    offsets = [(dx, dy) for dx in range(4) for dy in range(4)]
    offsets.sort(key=lambda o: min(o[0], 4 - o[0]) + min(o[1], 4 - o[1]))

    def feat_copy(piece, dx, dy):
        other = 4 * ((gx + dx) % 4) + (gy + dy) % 4
        return pltpu.make_async_remote_copy(
            src_ref=fsend.at[16 * piece + other],
            dst_ref=frecv.at[t],
            send_sem=feat_s,
            recv_sem=feat_r,
            device_id=(2 * other + c, row_of(piece)),
            device_id_type=MESH,
        )

    block_row = (z + 2) % 4
    scores_first(0, sbuf0)
    for pair in range(0, 8, 2):
        if pair == 6:
            project(3, 1)
        scores_first(pair + 1, sbuf1)
        attend_first(pair, sbuf0)
        if pair < 6:
            scores_first(pair + 2, sbuf0)
        attend_first(pair + 1, sbuf1)

    swap_keys(3).wait_recv()
    swap_values(3).wait_recv()
    def send_features(first, count):
        size = 128 * count
        at = slice(128 * first, 128 * first + size)
        own = hid[first : first + count].reshape(size, 1024).astype(F32)
        mixed = own + dot(attn[at, :], wo[...])
        after = normalize(mixed).astype(BF)
        feat = featin[at, :] + dot(after, patt[...]) + cam_row
        blocks = 16 * count
        both = jnp.concatenate(
            [feat[:, :128].reshape(blocks, 8, 128), feat[:, 128:].reshape(blocks, 8, 128)], axis=1
        )
        fsend[16 * first : 16 * first + blocks] = both.astype(BF)
        for piece in range(first, first + count):
            for dx, dy in reversed(offsets[int(piece == 3) :]):
                feat_copy(piece, dx, dy).start()

    scores_merge(0, abuf0)
    for pair in range(0, 8, 2):
        scores_merge(pair + 1, abuf1)
        attend_merge(pair, abuf0)
        if pair < 6:
            scores_merge(pair + 2, abuf0)
        else:
            scores_last(0, bbuf0)
        attend_merge(pair + 1, abuf1)

    send_features(0, 3)
    for pair in range(0, 8, 2):
        scores_last(pair + 1, bbuf1)
        attend_last(pair, bbuf0)
        if pair < 6:
            scores_last(pair + 2, bbuf0)
        attend_last(pair + 1, bbuf1)

    send_features(3, 1)
    pltpu.make_async_copy(fsend.at[48 + j], frecv.at[t], feat_r).start()

    pltpu.make_async_copy(frecv, frecv, feat_r).wait()

    got = frecv[...].astype(F32)
    got = jnp.concatenate(
        [got[:, :8, :].reshape(512, 128), got[:, 8:, :].reshape(512, 128)], axis=1
    ).astype(BF)
    feat = dot(perm[...], got)
    y = normalize(feat).astype(BF)
    tq = dot(y, tqw[...]) * (LOG2E / math.sqrt(32.0))
    tkv = dot(y, tkvw[...]).astype(BF)
    same = rows((512, 128)) // 64 % 2 == lanes((512, 128)) // 64
    head = lanes((128, 128)) // 32
    ones_t = jnp.ones((128, 128), BF)
    for b in range(4):
        for g in range(2):
            at = slice(128 * b, 128 * b + 128)
            col = slice(128 * g, 128 * g + 128)
            qb = tq[at, col]
            q4 = jnp.concatenate(
                [jnp.where(head == h, qb, 0.0).astype(BF) for h in range(4)], axis=0
            )
            s = lax.dot_general(q4, tkv[at, col], NT, preferred_element_type=F32)
            s = jnp.where(same, s, -jnp.inf)
            p = jnp.exp2(s - jnp.max(s, axis=-1, keepdims=True)).astype(BF)
            v = tkv[at, 256 + 128 * g : 384 + 128 * g]
            o = dot(p, jnp.concatenate([v, ones_t], axis=1))
            num = o[:128, :128]
            den = o[:128, 128:]
            for h in range(1, 4):
                num = jnp.where(head == h, o[128 * h : 128 * h + 128, :128], num)
                den = jnp.where(head == h, o[128 * h : 128 * h + 128, 128:], den)
            tattn[at, col] = (num / den).astype(BF)
    latent = feat + dot(tattn[...], toutw[...])
    logit = jnp.sum(latent * dread_ref[...], axis=-1, keepdims=True)

    lane = lanes((64, 128))
    block = jnp.zeros((64, 128), F32)
    for p in range(8):
        block = jnp.where(lane == 8 * j + p, logit[64 * p : 64 * p + 64, :], block)
    depth = 0.1 + jnp.maximum(block, 0.0) + jnp.log(1.0 + jnp.exp(-jnp.abs(block)))
    log_depth = jnp.dot(
        spread[...], jnp.log(depth), precision=lax.Precision.HIGHEST, preferred_element_type=F32
    )

    pltpu.make_async_copy(lall, lall, lid_r).wait()
    pixel = lall[:, :8, :].reshape(256, 128).astype(jnp.int32) - (256 * block_row + 128 * c)
    hit = (pixel >= 8 * j) & (pixel < 8 * j + 8)
    predicted = jnp.take_along_axis(log_depth, jnp.clip(pixel, 0, 127), axis=1)
    error = jnp.abs(predicted - lall[:, 8:, :].reshape(256, 128))
    partial = jnp.sum(jnp.where(hit, error, 0.0))

    mixed_out = jnp.where(lane // 8 == j, depth, partial)
    for k in range(64):
        dsend[k] = mixed_out[k : k + 1, :]

    slot = 2 * (16 * (2 * block_row + c) + j)

    def depth_copy(ff, zz):
        return pltpu.make_async_remote_copy(
            src_ref=dsend.at[pl.ds(2 * ff, 2)],
            dst_ref=drecv.at[pl.ds(slot, 2)],
            send_sem=dep_s,
            recv_sem=dep_r,
            device_id=(ff, zz),
            device_id_type=MESH,
        )

    def hops(offset):
        return sum(min(d, 4 - d) for d in offset[:3])

    everyone = [
        (dx, dy, dz, dc)
        for dx in range(4) for dy in range(4) for dz in range(4) for dc in range(2)
    ][1:]
    for dx, dy, dz, dc in sorted(everyone, key=hops, reverse=True):
        depth_copy(
            8 * ((gx + dx) % 4) + 2 * ((gy + dy) % 4) + (c + dc) % 2, (z + dz) % 4
        ).start()
    pltpu.make_async_copy(dsend.at[pl.ds(2 * f, 2)], drecv.at[pl.ds(slot, 2)], dep_r).start()

    pltpu.make_async_copy(drecv, drecv, dep_r).wait()

    group = lanes((1, 128)) // 8
    total = jnp.zeros((1, 128), F32)
    for b in range(8):
        acc = [jnp.zeros((1, 128), F32) for _ in range(2)]
        for jj in range(16):
            for i in range(2):
                part = drecv[2 * (16 * b + jj) + i]
                acc[i] = jnp.where(group == jj, part, acc[i])
                if i == 0:
                    total = total + jnp.where(group == (jj + 1) % 16, part, 0.0)
        for i in range(2):
            dfull[2 * b + i] = acc[i]
    for h in range(2):
        for i in range(2):
            depth_ref[i : i + 1, 128 * h : 128 * h + 128] = dfull[2 * (2 * z + h) + i]
    loss_ref[...] = jnp.sum(total, axis=-1, keepdims=True) * (1.0 / (8 * 64 * 512))

    pixel = lsend[:8, :].astype(jnp.int32)
    odd = rows((8, 128)) % 2 == 1
    found = jnp.ones((8, 128), F32)
    for b in range(8):
        table = jnp.where(
            odd,
            jnp.broadcast_to(dfull[2 * b + 1], (8, 128)),
            jnp.broadcast_to(dfull[2 * b], (8, 128)),
        )
        local = pixel - 128 * b
        value = jnp.take_along_axis(table, jnp.clip(local, 0, 127), axis=1)
        found = jnp.where((local >= 0) & (local < 128), value, found)
    error = jnp.where(pixel >= 0, jnp.log(found) - lsend[8:, :], 0.0)
    for k in range(4):
        perr_ref[:, 128 * k : 128 * k + 128] = error[2 * k : 2 * k + 2, :]

    for i, h in pieces:

        @pl.when(is_far(i))
        def _():
            piece_copy(i, h).wait_send()

    for piece in range(4):
        swap_keys(piece).wait_send()
        swap_values(piece).wait_send()
    pltpu.make_async_copy(lall.at[pl.ds(0, 31)], lall.at[pl.ds(0, 31)], lid_s).wait()
    pltpu.make_async_copy(frecv.at[pl.ds(0, 63)], frecv.at[pl.ds(0, 63)], feat_s).wait()
    pltpu.make_async_copy(drecv.at[pl.ds(0, 254)], drecv.at[pl.ds(0, 254)], dep_s).wait()


def pass_on(depth_in, perr_in, loss_in, depth_out, perr_out, loss_out, sem):
    pairs = [(depth_in, depth_out), (perr_in, perr_out), (loss_in, loss_out)]
    copies = [pltpu.make_async_copy(a, b, sem.at[k]) for k, (a, b) in enumerate(pairs)]
    for copy in copies:
        copy.start()
    for copy in copies:
        copy.wait()


def body(
    hidden_in, query_weight, kv_weight, out_weight, proj_in, proj_attn, camera_table, camera_id,
    t_query, t_kv, t_out, depth_read, lidar_pixel, lidar_depth, lidar_valid,
):
    hbm = pl.BlockSpec(memory_space=pl.ANY)
    vmem = pl.BlockSpec(memory_space=pltpu.VMEM)
    smem = pl.BlockSpec(memory_space=pltpu.SMEM)
    dma = pltpu.SemaphoreType.DMA
    depth_map, point_error, loss = pl.pallas_call(
        kernel,
        out_shape=(
            jax.ShapeDtypeStruct((2, 256), F32),
            jax.ShapeDtypeStruct((2, 512), F32),
            jax.ShapeDtypeStruct((1, 1), F32),
        ),
        in_specs=[
            hbm, hbm, hbm, hbm, hbm, hbm, vmem, smem, hbm, hbm, hbm, vmem, vmem, vmem, vmem,
        ],
        out_specs=(vmem, vmem, vmem),
        scratch_shapes=[
            pltpu.VMEM((4, 128, 1024), BF),
            pltpu.VMEM((1024, 1024), BF),
            pltpu.VMEM((1024, 2048), BF),
            pltpu.VMEM((1024, 1024), BF),
            pltpu.VMEM((1024, 256), BF),
            pltpu.VMEM((1024, 256), BF),
            pltpu.VMEM((256, 256), BF),
            pltpu.VMEM((256, 512), BF),
            pltpu.VMEM((256, 256), BF),
            pltpu.VMEM((512, 1024), BF),
            pltpu.VMEM((2, 512, 1024), BF),
            pltpu.VMEM((8, 1024, 128), BF),
            pltpu.VMEM((1024, 1024), BF),
            pltpu.VMEM((768, 768), F32),
            pltpu.VMEM((768, 768), F32),
            pltpu.VMEM((768, 256), F32),
            pltpu.VMEM((768, 256), F32),
            pltpu.VMEM((256, 1024), F32),
            pltpu.VMEM((256, 1024), F32),
            pltpu.VMEM((8, 768, 256), F32),
            pltpu.VMEM((8, 768, 128), F32),
            pltpu.VMEM((512, 1024), BF),
            pltpu.VMEM((512, 256), F32),
            pltpu.VMEM((64, 16, 128), BF),
            pltpu.VMEM((64, 16, 128), BF),
            pltpu.VMEM((512, 512), BF),
            pltpu.VMEM((256, 64), F32),
            pltpu.VMEM((512, 256), BF),
            pltpu.VMEM((16, 128), F32),
            pltpu.VMEM((32, 16, 128), F32),
            pltpu.VMEM((64, 1, 128), F32),
            pltpu.VMEM((256, 1, 128), F32),
            pltpu.VMEM((16, 1, 128), F32),
            pltpu.SemaphoreType.REGULAR, pltpu.SemaphoreType.REGULAR,
            dma((8,)), dma((4,)), dma((4,)), dma((2, 4)), dma((2, 4)),
            dma, dma, dma, dma, dma, dma,
        ],
        compiler_params=pltpu.CompilerParams(
            collective_id=0, has_side_effects=True, vmem_limit_bytes=56 * 2**20
        ),
        cost_estimate=pl.CostEstimate(
            flops=8_000_000_000, bytes_accessed=12_000_000, transcendentals=9_000_000
        ),
    )(
        hidden_in, query_weight, kv_weight, out_weight, proj_in, proj_attn, camera_table,
        camera_id, t_query, t_kv, t_out, depth_read.reshape(1, -1), lidar_pixel, lidar_depth,
        lidar_valid,
    )
    depth_map, point_error, loss = pl.pallas_call(
        pass_on,
        out_shape=(
            jax.ShapeDtypeStruct((2, 256), F32),
            jax.ShapeDtypeStruct((2, 512), F32),
            jax.ShapeDtypeStruct((1, 1), F32),
        ),
        in_specs=[hbm, hbm, hbm],
        out_specs=(hbm, hbm, hbm),
        scratch_shapes=[dma((3,))],
    )(depth_map, point_error, loss)
    return depth_map, point_error, loss.reshape(())


def solution(mesh):
    return jax.shard_map(
        body,
        mesh=mesh,
        in_specs=(
            P("frame", "row", None),
            P(),
            P(),
            P(),
            P(),
            P(),
            P(),
            P(),
            P(),
            P(),
            P(),
            P(),
            P("frame", None),
            P("frame", None),
            P("frame", None),
        ),
        out_specs=(P("frame", "row"), P("frame", None), P()),
        check_vma=False,
    )
```

```python
import functools
import math

import jax
import jax.numpy as jnp
from jax import lax
from jax.experimental import pallas as pl
from jax.experimental.pallas import tpu as pltpu
from jax.sharding import PartitionSpec as P

MESH = pl.DeviceIdType.MESH
BF = jnp.bfloat16
F32 = jnp.float32
LOG2E = 1.4426950408889634
T_HEADS = 8
CAMERAS = 6
NT = (((1,), (1,)), ((), ()))


def normalize(values):
    mean = jnp.mean(values, axis=-1, keepdims=True)
    centred = values - mean
    var = jnp.mean(centred * centred, axis=-1, keepdims=True)
    return centred * lax.rsqrt(var + 1e-06)


def dot(a, b):
    return jnp.dot(a, b, preferred_element_type=F32)


def lanes(shape):
    return lax.broadcasted_iota(jnp.int32, shape, len(shape) - 1)


def rows(shape):
    return lax.broadcasted_iota(jnp.int32, shape, len(shape) - 2)


def kernel(
    x_ref, wq_h, wkv_h, wo_h, pin_h, patt_h, cam_ref, cid_ref, tq_h, tkv_h, tout_h, dread_ref,
    lpix_ref, ldep_ref, lval_ref,
    depth_ref, perr_ref, loss_ref,
    hid, wq, wkv, wo, pin, patt, tqw, tkvw, toutw,
    normed, qm, ktbuf, vbuf, sbuf0, sbuf1, abuf0, abuf1, bbuf0, bbuf1, obuf, mbuf, attn, featin, fsend, frecv,
    perm, spread, tattn, lsend, lall, dsend, drecv, dfull,
    here_x, here_y, wsem, hid_s, hid_r, kv_s, kv_r, lid_s, lid_r, feat_s, feat_r, dep_s, dep_r,
):
    f = lax.axis_index("frame")
    z = lax.axis_index("row")
    j = f // 2
    c = f % 2
    t = 4 * j + z

    barrier = pltpu.get_barrier_semaphore()

    gx, gy = f // 8, j % 4
    column = [(2 * j + (c + dc) % 2, (z + dz) % 4) for dz in range(4) for dc in range(2)][1:]
    along_x = [(8 * ((gx + d) % 4) + 2 * gy + c, z) for d in range(1, 4)]
    along_y = [(8 * gx + 2 * ((gy + d) % 4) + c, z) for d in range(1, 4)]
    for device in column + along_x + along_y:
        pl.semaphore_signal(barrier, inc=1, device_id=device, device_id_type=MESH)

    weights = [
        pltpu.make_async_copy(src, dst, wsem.at[k])
        for k, (src, dst) in enumerate(
            [(wkv_h, wkv), (wq_h, wq), (pin_h, pin), (wo_h, wo), (patt_h, patt),
             (tq_h, tqw), (tkv_h, tkvw), (tout_h, toutw)]
        )
    ]
    for copy in weights:
        copy.start()

    for k in range(4):
        part = slice(128 * k, 128 * k + 128)
        pixel = jnp.where(lval_ref[:, part] != 0, lpix_ref[:, part], -1).astype(F32)
        lsend[2 * k : 2 * k + 2, :] = pixel
        lsend[8 + 2 * k : 10 + 2 * k, :] = jnp.log(ldep_ref[:, part])
    own_points = pltpu.make_async_copy(lsend, lall.at[f], lid_r)
    own_points.start()

    pl.semaphore_wait(barrier, 13)

    def slot_of(i):
        far = (z - 2 * c - i + 4) % 4
        return jnp.where(far == 2, 3, jnp.where(far == 3, 2, far))

    def piece_copy(i, h):
        return pltpu.make_async_remote_copy(
            src_ref=x_ref.at[i, pl.ds(128 * h, 128)],
            dst_ref=hid.at[slot_of(i)],
            send_sem=hid_s.at[2 * i + h],
            recv_sem=hid_r.at[slot_of(i)],
            device_id=(2 * j + h, 2 * c + i),
            device_id_type=MESH,
        )

    def piece_here(i, h):
        return (2 * c + i == z) & (h == c)

    pieces = [(i, h) for i in range(2) for h in range(2)]

    def is_far(i):
        return (2 * c + i - z + 4) % 4 == 2

    for i, h in pieces:

        @pl.when(jnp.logical_not(piece_here(i, h) | is_far(i)))
        def _():
            piece_copy(i, h).start()

    for i, h in pieces:

        @pl.when(piece_here(i, h))
        def _():
            pltpu.make_async_copy(
                x_ref.at[i, pl.ds(128 * h, 128)], hid.at[0], hid_r.at[0]
            ).start()

    for device in along_x:
        pl.semaphore_signal(here_x, inc=1, device_id=device, device_id_type=MESH)

    row = rows((512, 512))
    perm[...] = jnp.where(lanes((512, 512)) == (row % 64) * 8 + row // 64, 1.0, 0.0).astype(BF)
    row = rows((256, 64))
    spread[...] = jnp.where(lanes((256, 64)) == 2 * (row // 8) + row % 2, 1.0, 0.0)

    pl.semaphore_wait(here_x, 3)
    for device in along_y:
        pl.semaphore_signal(here_y, inc=1, device_id=device, device_id_type=MESH)

    def swap_keys(piece):
        return pltpu.make_async_remote_copy(
            src_ref=ktbuf.at[2 * piece],
            dst_ref=ktbuf.at[2 * piece + 1],
            send_sem=kv_s.at[0, piece],
            recv_sem=kv_r.at[0, piece],
            device_id=(2 * j + 1 - c, z),
            device_id_type=MESH,
        )

    def swap_values(piece):
        return pltpu.make_async_remote_copy(
            src_ref=vbuf.at[pl.ds(256 * piece, 128)],
            dst_ref=vbuf.at[pl.ds(256 * piece + 128, 128)],
            send_sem=kv_s.at[1, piece],
            recv_sem=kv_r.at[1, piece],
            device_id=(2 * j + 1 - c, z),
            device_id_type=MESH,
        )

    for copy in weights[:3]:
        copy.wait()

    def points_copy(ff):
        return pltpu.make_async_remote_copy(
            src_ref=lsend,
            dst_ref=lall.at[f],
            send_sem=lid_s,
            recv_sem=lid_r,
            device_id=(ff, z),
            device_id_type=MESH,
        )

    def project(first, count):
        for piece in range(first, first + count):
            pltpu.make_async_copy(hid.at[piece], hid.at[piece], hid_r.at[piece]).wait()
        size = 128 * count
        at = slice(128 * first, 128 * first + size)
        own = hid[first : first + count].reshape(size, 1024)
        normed[at, :] = normalize(own.astype(F32)).astype(BF)
        key = dot(normed[at, :], wkv[:, :1024]).astype(BF)
        for k in range(count):
            ktbuf[2 * (first + k)] = key[128 * k : 128 * k + 128].T
            swap_keys(first + k).start()
        value = dot(normed[at, :], wkv[:, 1024:]).astype(BF)
        for k in range(count):
            row = 256 * (first + k)
            vbuf[row : row + 128, :] = value[128 * k : 128 * k + 128]
            swap_values(first + k).start()
        q = dot(normed[at, :], wq[...]) * (LOG2E / 8.0)
        low = lanes((size, 1024)) % 128 < 64
        qm[0, at, :] = jnp.where(low, q, 0.0).astype(BF)
        qm[1, at, :] = jnp.where(low, 0.0, q).astype(BF)
        featin[at, :] = dot(normed[at, :], pin[...])

    project(0, 1)
    pl.semaphore_wait(here_y, 3)

    @pl.loop(1, 32)
    def _(ff):
        points_copy((f + ff) % 32).start()

    for i, h in pieces:

        @pl.when(jnp.logical_not(piece_here(i, h) | is_far(i)))
        def _():
            piece_copy(i, h).wait_send()

    for i, h in pieces:

        @pl.when(is_far(i))
        def _():
            piece_copy(i, h).start()

    project(1, 2)

    camera = cid_ref[t]
    cam_row = jnp.zeros((1, 256), F32)
    for k in range(CAMERAS):
        cam_row = cam_row + cam_ref[k : k + 1, :].astype(F32) * jnp.where(camera == k, 1.0, 0.0)

    for piece in range(3):
        swap_keys(piece).wait_recv()

    def at_pair(pair):
        return pl.ds(128 * pair if isinstance(pair, int) else pl.multiple_of(128 * pair, 128), 128)

    def keys_of(first, last, col):
        return jnp.concatenate([ktbuf[k, col, :] for k in range(first, last)], axis=1)

    def scores_first(pair, out):
        col = at_pair(pair)
        q2 = qm[:, :384, col].reshape(768, 128)
        out[...] = dot(q2, keys_of(0, 6, col))

    def values(at, col, count):
        return jnp.concatenate([vbuf[at, col], jnp.ones((count, 128), BF)], axis=1)

    def attend_first(pair, s_ref):
        col = at_pair(pair)
        s = s_ref[...]
        top = jnp.max(s, axis=-1, keepdims=True)
        p = jnp.exp2((s - top).astype(BF))
        obuf[pair] = dot(p, values(slice(0, 768), col, 768))
        mbuf[pair] = jnp.broadcast_to(top, (768, 128))

    def scores_merge(pair, out):
        col = at_pair(pair)
        q2 = qm[:, :384, col].reshape(768, 128)
        out[...] = dot(q2, keys_of(6, 8, col))

    def scores_last(pair, out):
        col = at_pair(pair)
        q2 = qm[:, 384:, col].reshape(256, 128)
        out[...] = dot(q2, keys_of(0, 8, col))

    def heads_of(o, count):
        left = lanes((count, 128)) < 64
        num = jnp.where(left, o[:count, :128], o[count:, :128])
        den = jnp.where(left, o[:count, 128:], o[count:, 128:])
        return (num / den).astype(BF)

    def attend_merge(pair, s_ref):
        col = at_pair(pair)
        s = s_ref[...]
        before = mbuf[pair]
        top = jnp.maximum(before, jnp.max(s, axis=-1, keepdims=True))
        p = jnp.exp2((s - jnp.concatenate([top, top], axis=1)).astype(BF))
        keep = jnp.exp2(before - top)
        o = obuf[pair] * jnp.concatenate([keep, keep], axis=1)
        o = o + dot(p, values(slice(768, 1024), col, 256))
        attn[:384, col] = heads_of(o, 384)

    def attend_last(pair, s_ref):
        col = at_pair(pair)
        s = s_ref[...]
        p = jnp.exp2((s - jnp.max(s, axis=-1, keepdims=True)).astype(BF))
        attn[384:, col] = heads_of(dot(p, values(slice(0, 1024), col, 1024)), 128)

    def row_of(piece):
        return (z + 2 + (0, 1, 3, 2)[piece]) % 4

    offsets = [(dx, dy) for dx in range(4) for dy in range(4)]
    offsets.sort(key=lambda o: min(o[0], 4 - o[0]) + min(o[1], 4 - o[1]))

    def feat_copy(piece, dx, dy):
        other = 4 * ((gx + dx) % 4) + (gy + dy) % 4
        return pltpu.make_async_remote_copy(
            src_ref=fsend.at[16 * piece + other],
            dst_ref=frecv.at[t],
            send_sem=feat_s,
            recv_sem=feat_r,
            device_id=(2 * other + c, row_of(piece)),
            device_id_type=MESH,
        )

    block_row = (z + 2) % 4
    scores_first(0, sbuf0)
    for piece in range(3):
        swap_values(piece).wait_recv()
    for pair in range(0, 8, 2):
        if pair == 6:
            project(3, 1)
        scores_first(pair + 1, sbuf1)
        attend_first(pair, sbuf0)
        if pair < 6:
            scores_first(pair + 2, sbuf0)
        attend_first(pair + 1, sbuf1)

    swap_keys(3).wait_recv()
    def send_features(first, count):
        size = 128 * count
        at = slice(128 * first, 128 * first + size)
        own = hid[first : first + count].reshape(size, 1024).astype(F32)
        mixed = own + dot(attn[at, :], wo[...])
        after = normalize(mixed).astype(BF)
        feat = featin[at, :] + dot(after, patt[...]) + cam_row
        blocks = 16 * count
        both = jnp.concatenate(
            [feat[:, :128].reshape(blocks, 8, 128), feat[:, 128:].reshape(blocks, 8, 128)], axis=1
        )
        fsend[16 * first : 16 * first + blocks] = both.astype(BF)
        for piece in range(first, first + count):
            for dx, dy in reversed(offsets[int(piece == 3) :]):
                feat_copy(piece, dx, dy).start()

    scores_merge(0, abuf0)
    swap_values(3).wait_recv()
    for copy in weights[3:]:
        copy.wait()
    for pair in range(0, 8, 2):
        scores_merge(pair + 1, abuf1)
        attend_merge(pair, abuf0)
        if pair < 6:
            scores_merge(pair + 2, abuf0)
        else:
            scores_last(0, bbuf0)
        attend_merge(pair + 1, abuf1)

    send_features(0, 3)
    for pair in range(0, 8, 2):
        scores_last(pair + 1, bbuf1)
        attend_last(pair, bbuf0)
        if pair < 6:
            scores_last(pair + 2, bbuf0)
        attend_last(pair + 1, bbuf1)

    send_features(3, 1)
    pltpu.make_async_copy(fsend.at[48 + j], frecv.at[t], feat_r).start()

    pltpu.make_async_copy(frecv, frecv, feat_r).wait()

    got = frecv[...].astype(F32)
    got = jnp.concatenate(
        [got[:, :8, :].reshape(512, 128), got[:, 8:, :].reshape(512, 128)], axis=1
    ).astype(BF)
    feat = dot(perm[...], got)
    y = normalize(feat).astype(BF)
    tq = dot(y, tqw[...]) * (LOG2E / math.sqrt(32.0))
    tkv = dot(y, tkvw[...]).astype(BF)
    same = rows((512, 128)) // 64 % 2 == lanes((512, 128)) // 64
    head = lanes((128, 128)) // 32
    ones_t = jnp.ones((128, 128), BF)
    for b in range(4):
        for g in range(2):
            at = slice(128 * b, 128 * b + 128)
            col = slice(128 * g, 128 * g + 128)
            qb = tq[at, col]
            q4 = jnp.concatenate(
                [jnp.where(head == h, qb, 0.0).astype(BF) for h in range(4)], axis=0
            )
            s = lax.dot_general(q4, tkv[at, col], NT, preferred_element_type=F32)
            s = jnp.where(same, s, -jnp.inf)
            p = jnp.exp2(s - jnp.max(s, axis=-1, keepdims=True)).astype(BF)
            v = tkv[at, 256 + 128 * g : 384 + 128 * g]
            o = dot(p, jnp.concatenate([v, ones_t], axis=1))
            num = o[:128, :128]
            den = o[:128, 128:]
            for h in range(1, 4):
                num = jnp.where(head == h, o[128 * h : 128 * h + 128, :128], num)
                den = jnp.where(head == h, o[128 * h : 128 * h + 128, 128:], den)
            tattn[at, col] = (num / den).astype(BF)
    latent = feat + dot(tattn[...], toutw[...])
    logit = jnp.sum(latent * dread_ref[...], axis=-1, keepdims=True)

    lane = lanes((64, 128))
    block = jnp.zeros((64, 128), F32)
    for p in range(8):
        block = jnp.where(lane == 8 * j + p, logit[64 * p : 64 * p + 64, :], block)
    depth = 0.1 + jnp.maximum(block, 0.0) + jnp.log(1.0 + jnp.exp(-jnp.abs(block)))
    log_depth = jnp.dot(
        spread[...], jnp.log(depth), precision=lax.Precision.HIGHEST, preferred_element_type=F32
    )

    pltpu.make_async_copy(lall, lall, lid_r).wait()
    pixel = lall[:, :8, :].reshape(256, 128).astype(jnp.int32) - (256 * block_row + 128 * c)
    hit = (pixel >= 8 * j) & (pixel < 8 * j + 8)
    predicted = jnp.take_along_axis(log_depth, jnp.clip(pixel, 0, 127), axis=1)
    error = jnp.abs(predicted - lall[:, 8:, :].reshape(256, 128))
    partial = jnp.sum(jnp.where(hit, error, 0.0))

    mixed_out = jnp.where(lane // 8 == j, depth, partial)
    for k in range(64):
        dsend[k] = mixed_out[k : k + 1, :]

    slot = 2 * (16 * (2 * block_row + c) + j)

    def depth_copy(ff, zz):
        return pltpu.make_async_remote_copy(
            src_ref=dsend.at[pl.ds(2 * ff, 2)],
            dst_ref=drecv.at[pl.ds(slot, 2)],
            send_sem=dep_s,
            recv_sem=dep_r,
            device_id=(ff, zz),
            device_id_type=MESH,
        )

    def hops(offset):
        return sum(min(d, 4 - d) for d in offset[:3])

    everyone = [
        (dx, dy, dz, dc)
        for dx in range(4) for dy in range(4) for dz in range(4) for dc in range(2)
    ][1:]
    for dx, dy, dz, dc in sorted(everyone, key=hops, reverse=True):
        depth_copy(
            8 * ((gx + dx) % 4) + 2 * ((gy + dy) % 4) + (c + dc) % 2, (z + dz) % 4
        ).start()
    pltpu.make_async_copy(dsend.at[pl.ds(2 * f, 2)], drecv.at[pl.ds(slot, 2)], dep_r).start()

    pltpu.make_async_copy(drecv, drecv, dep_r).wait()

    group = lanes((1, 128)) // 8
    total = jnp.zeros((1, 128), F32)
    for b in range(8):
        acc = [jnp.zeros((1, 128), F32) for _ in range(2)]
        for jj in range(16):
            for i in range(2):
                part = drecv[2 * (16 * b + jj) + i]
                acc[i] = jnp.where(group == jj, part, acc[i])
                if i == 0:
                    total = total + jnp.where(group == (jj + 1) % 16, part, 0.0)
        for i in range(2):
            dfull[2 * b + i] = acc[i]
    for h in range(2):
        for i in range(2):
            depth_ref[i : i + 1, 128 * h : 128 * h + 128] = dfull[2 * (2 * z + h) + i]
    loss_ref[...] = jnp.sum(total, axis=-1, keepdims=True) * (1.0 / (8 * 64 * 512))

    pixel = lsend[:8, :].astype(jnp.int32)
    odd = rows((8, 128)) % 2 == 1
    found = jnp.ones((8, 128), F32)
    for b in range(8):
        table = jnp.where(
            odd,
            jnp.broadcast_to(dfull[2 * b + 1], (8, 128)),
            jnp.broadcast_to(dfull[2 * b], (8, 128)),
        )
        local = pixel - 128 * b
        value = jnp.take_along_axis(table, jnp.clip(local, 0, 127), axis=1)
        found = jnp.where((local >= 0) & (local < 128), value, found)
    error = jnp.where(pixel >= 0, jnp.log(found) - lsend[8:, :], 0.0)
    for k in range(4):
        perr_ref[:, 128 * k : 128 * k + 128] = error[2 * k : 2 * k + 2, :]

    for i, h in pieces:

        @pl.when(is_far(i))
        def _():
            piece_copy(i, h).wait_send()

    for piece in range(4):
        swap_keys(piece).wait_send()
        swap_values(piece).wait_send()
    pltpu.make_async_copy(lall.at[pl.ds(0, 31)], lall.at[pl.ds(0, 31)], lid_s).wait()
    pltpu.make_async_copy(frecv.at[pl.ds(0, 63)], frecv.at[pl.ds(0, 63)], feat_s).wait()
    pltpu.make_async_copy(drecv.at[pl.ds(0, 254)], drecv.at[pl.ds(0, 254)], dep_s).wait()


def pass_on(depth_in, perr_in, loss_in, depth_out, perr_out, loss_out, sem):
    pairs = [(depth_in, depth_out), (perr_in, perr_out), (loss_in, loss_out)]
    copies = [pltpu.make_async_copy(a, b, sem.at[k]) for k, (a, b) in enumerate(pairs)]
    for copy in copies:
        copy.start()
    for copy in copies:
        copy.wait()


def body(
    hidden_in, query_weight, kv_weight, out_weight, proj_in, proj_attn, camera_table, camera_id,
    t_query, t_kv, t_out, depth_read, lidar_pixel, lidar_depth, lidar_valid,
):
    hbm = pl.BlockSpec(memory_space=pl.ANY)
    vmem = pl.BlockSpec(memory_space=pltpu.VMEM)
    smem = pl.BlockSpec(memory_space=pltpu.SMEM)
    dma = pltpu.SemaphoreType.DMA
    depth_map, point_error, loss = pl.pallas_call(
        kernel,
        out_shape=(
            jax.ShapeDtypeStruct((2, 256), F32),
            jax.ShapeDtypeStruct((2, 512), F32),
            jax.ShapeDtypeStruct((1, 1), F32),
        ),
        in_specs=[
            hbm, hbm, hbm, hbm, hbm, hbm, vmem, smem, hbm, hbm, hbm, vmem, vmem, vmem, vmem,
        ],
        out_specs=(vmem, vmem, vmem),
        scratch_shapes=[
            pltpu.VMEM((4, 128, 1024), BF),
            pltpu.VMEM((1024, 1024), BF),
            pltpu.VMEM((1024, 2048), BF),
            pltpu.VMEM((1024, 1024), BF),
            pltpu.VMEM((1024, 256), BF),
            pltpu.VMEM((1024, 256), BF),
            pltpu.VMEM((256, 256), BF),
            pltpu.VMEM((256, 512), BF),
            pltpu.VMEM((256, 256), BF),
            pltpu.VMEM((512, 1024), BF),
            pltpu.VMEM((2, 512, 1024), BF),
            pltpu.VMEM((8, 1024, 128), BF),
            pltpu.VMEM((1024, 1024), BF),
            pltpu.VMEM((768, 768), F32),
            pltpu.VMEM((768, 768), F32),
            pltpu.VMEM((768, 256), F32),
            pltpu.VMEM((768, 256), F32),
            pltpu.VMEM((256, 1024), F32),
            pltpu.VMEM((256, 1024), F32),
            pltpu.VMEM((8, 768, 256), F32),
            pltpu.VMEM((8, 768, 128), F32),
            pltpu.VMEM((512, 1024), BF),
            pltpu.VMEM((512, 256), F32),
            pltpu.VMEM((64, 16, 128), BF),
            pltpu.VMEM((64, 16, 128), BF),
            pltpu.VMEM((512, 512), BF),
            pltpu.VMEM((256, 64), F32),
            pltpu.VMEM((512, 256), BF),
            pltpu.VMEM((16, 128), F32),
            pltpu.VMEM((32, 16, 128), F32),
            pltpu.VMEM((64, 1, 128), F32),
            pltpu.VMEM((256, 1, 128), F32),
            pltpu.VMEM((16, 1, 128), F32),
            pltpu.SemaphoreType.REGULAR, pltpu.SemaphoreType.REGULAR,
            dma((8,)), dma((4,)), dma((4,)), dma((2, 4)), dma((2, 4)),
            dma, dma, dma, dma, dma, dma,
        ],
        compiler_params=pltpu.CompilerParams(
            collective_id=0, has_side_effects=True, vmem_limit_bytes=56 * 2**20
        ),
        cost_estimate=pl.CostEstimate(
            flops=8_000_000_000, bytes_accessed=12_000_000, transcendentals=9_000_000
        ),
    )(
        hidden_in, query_weight, kv_weight, out_weight, proj_in, proj_attn, camera_table,
        camera_id, t_query, t_kv, t_out, depth_read.reshape(1, -1), lidar_pixel, lidar_depth,
        lidar_valid,
    )
    depth_map, point_error, loss = pl.pallas_call(
        pass_on,
        out_shape=(
            jax.ShapeDtypeStruct((2, 256), F32),
            jax.ShapeDtypeStruct((2, 512), F32),
            jax.ShapeDtypeStruct((1, 1), F32),
        ),
        in_specs=[hbm, hbm, hbm],
        out_specs=(hbm, hbm, hbm),
        scratch_shapes=[dma((3,))],
    )(depth_map, point_error, loss)
    return depth_map, point_error, loss.reshape(())


def solution(mesh):
    return jax.shard_map(
        body,
        mesh=mesh,
        in_specs=(
            P("frame", "row", None),
            P(),
            P(),
            P(),
            P(),
            P(),
            P(),
            P(),
            P(),
            P(),
            P(),
            P(),
            P("frame", None),
            P("frame", None),
            P("frame", None),
        ),
        out_specs=(P("frame", "row"), P("frame", None), P()),
        check_vma=False,
    )
```
